768 devices in a mesh: fsdp: 12 (over z_hi, x), tensor: 64 (over z_lo, y, core).
Axes of the slice: x: 4, y: 8, z: 12 (z_hi: 3, z_lo: 4; z = z_hi * 4 + z_lo), core: 2. Of those that a mesh axis runs over, the one named last changes fastest.
Arguments:
- hidden: bfloat16 [1536, 53248], P('fsdp', 'tensor'), may hold values from -6 to 6
- down_weight: bfloat16 [53248, 12288], P('tensor', 'fsdp'), may hold values from -0.02734375 to 0.02734375
- act_exponent: int32 [1536, 832], P('fsdp', 'tensor'), may hold values from -2 to 0
- clip_index: int32 [832], P('tensor'), may hold values from 0 to 3
- weight_exponent: int32 [12288], P('fsdp'), may hold values from -9 to -8
Outputs:
- projected: bfloat16 [1536, 12288], P('tensor', 'fsdp')
The draws below stay inside these ranges and needn't reach their ends.
All inputs are finite; a program needn't handle non-finite values.
Results may differ from the reference program's by a relative error of at most 0.0053.
Values may be sent and summed in bfloat16 or wider, within the bound.
No kernel may reach another device: no remote copies, remote signals or barrier semaphores. Data moves between devices by JAX's collectives and lax.ppermute only.
A program may use at most 32 MiB of HBM per device.

```python
import math
import jax
import jax.numpy as jnp
from jax import lax

D = 12288
FF = 53248
TOKENS = 1536
GROUPS = 832
N_TENSOR = 64


def set_ends(values, own_key, least, largest):
    extent = values.shape
    index_at = [jax.random.randint(jax.random.fold_in(own_key, axis), (), 0, extent[axis]) for axis in range(len(extent))]
    values = values.at[tuple(index_at)].set(least)
    longest = extent.index(max(extent))
    index_at[longest] = (index_at[longest] + 1) % extent[longest]
    return values.at[tuple(index_at)].set(largest)


def steps_of(rng, dims, pieces, least, high):
    gain, own = 1.0, jax.random.fold_in(rng, 6)
    for axis_at, blocks in pieces:
        heights = jnp.exp(jax.random.uniform(jax.random.fold_in(own, axis_at), (blocks,), jnp.float32, least / len(pieces), high / len(pieces)))
        gain = gain * jnp.repeat(heights, dims[axis_at] // blocks).reshape([-1 if axis == axis_at else 1 for axis in range(len(dims))])
    return gain


def gaussian(key, dims, width, bound, split=(), kind=jnp.bfloat16):
    loudness = steps_of(key, dims, split, -0.22, 0.18) if split else 1.0
    entries = jax.random.normal(key, dims, jnp.float32) * width * loudness
    return jnp.minimum(jnp.maximum(entries, -bound), bound).astype(kind)


def setup_inputs(seed: int = 0) -> dict:
    keys = jax.random.split(jax.random.key(seed), 6)
    return {
        "hidden": gaussian(keys[0], (TOKENS, FF), 1.0, 6.0, ((0, 12), (1, 64))),
        "down_weight": gaussian(keys[1], (FF, D), FF ** -0.5, 0.02734375, ((0, 64), (1, 12))),
        "act_exponent": set_ends(jax.random.randint(keys[2], (TOKENS, GROUPS), -2, 1), jax.random.fold_in(keys[2], 1), -2, 0).astype(jnp.int32),
        "clip_index": set_ends(jax.random.randint(keys[3], (GROUPS,), 0, 4), jax.random.fold_in(keys[3], 1), 0, 3).astype(jnp.int32),
        "weight_exponent": set_ends(jax.random.randint(keys[4], (D,), -9, -7), jax.random.fold_in(keys[4], 1), -9, (-7) - 1).astype(jnp.int32),
    }


def walsh_matrix(order_size):
    indices = jnp.arange(order_size, dtype=jnp.int32)
    shared = indices[:, None] & indices[None, :]
    parity = jnp.zeros((order_size, order_size), jnp.int32)
    for bit_level in range(order_size.bit_length() - 1):
        parity = parity ^ shared >> bit_level & 1
    return (1 - 2 * parity).astype(jnp.float32)

def soft_round(values):
    return values - jnp.sin(2.0 * math.pi * values) / (2.0 * math.pi)

def quantize_rows(rotated, act_exponent, clip_index):
    row_count, unit_count = rotated.shape
    scaling = jnp.exp2(act_exponent.astype(jnp.float32))[:, :, None]
    clip_level = (7.5 - clip_index.astype(jnp.float32))[None, :, None]
    grouped = rotated.reshape(row_count, unit_count // 64, 64) / scaling
    clipped = jnp.clip(grouped, -clip_level, clip_level)
    return (soft_round(clipped) * scaling).reshape(row_count, unit_count).astype(jnp.bfloat16)

def quantize_weight(weight_matrix, weight_exponent):
    scaling = jnp.exp2(weight_exponent.astype(jnp.float32))[None, :]
    clipped = jnp.clip(weight_matrix.astype(jnp.float32) / scaling, -7.5, 7.5)
    return (soft_round(clipped) * scaling).astype(jnp.bfloat16)

def reference(hidden, down_weight, act_exponent, clip_index, weight_exponent):
    row_count = hidden.shape[0]
    tensor_size = N_TENSOR
    inner = FF // (tensor_size * 64)
    local_mixed = jnp.dot(hidden.reshape(-1, 64), walsh_matrix(64).astype(jnp.bfloat16), preferred_element_type=jnp.float32).reshape(row_count, tensor_size, inner, 64)
    normalizer = 1.0 / math.sqrt(64.0 * tensor_size)
    rotated = jnp.einsum('st,ktce->ksce', walsh_matrix(tensor_size), local_mixed, precision=lax.Precision.HIGHEST).reshape(row_count, FF) * normalizer
    quantized = quantize_rows(rotated, act_exponent, clip_index)
    block_rows = FF // tensor_size
    act_blocks = quantized.reshape(row_count, tensor_size, block_rows).transpose(1, 0, 2)
    weight_blocks = down_weight.reshape(tensor_size, block_rows, D)
    exps = weight_exponent

    def accumulate(total, pair):
        act_block, weight_block = pair
        weight_q = quantize_weight(weight_block, exps)
        return (total + jnp.dot(act_block, weight_q, preferred_element_type=jnp.float32), None)
    total, _ = lax.scan(accumulate, jnp.zeros((row_count, D), jnp.float32), (act_blocks, weight_blocks))
    return total.astype(jnp.bfloat16)
```

```python
import math

import jax
import jax.numpy as jnp
import numpy as np
from jax import lax
from jax.experimental import pallas as pl
from jax.experimental.pallas import tpu as pltpu
from jax.sharding import Mesh, PartitionSpec as P

AXES = ("h", "x", "l", "yh", "yl", "c")
SIZES = (3, 4, 4, 4, 2, 2)
TENSOR = ("l", "yh", "yl", "c")
SLOTS = (0, 1, 3, 2)
WIDTH = 896


def sine_coefficients():
    nodes = 0.25 * (1.0 + np.cos(np.pi * (np.arange(400) + 0.5) / 400)) ** 1.0
    squares = nodes**2
    target = np.sin(2.0 * np.pi * nodes) / (2.0 * np.pi)
    table = np.stack([nodes * squares**power for power in range(8)], axis=1)
    solved = np.linalg.lstsq(table, target, rcond=None)[0]
    return [float(entry) for entry in solved]


SINE = sine_coefficients()


def soft_round(values):
    rest = values - jnp.round(values)
    squares = rest * rest
    total = jnp.full_like(rest, SINE[-1])
    for entry in SINE[-2::-1]:
        total = total * squares + entry
    return values - rest * total


def walsh(order):
    indices = np.arange(order)
    shared = indices[:, None] & indices[None, :]
    parity = np.zeros((order, order), np.int64)
    for bit_level in range(order.bit_length() - 1):
        parity ^= shared >> bit_level & 1
    return (1 - 2 * parity).astype(np.float32)


def rotate_kernel(x_ref, rows_ref, lanes_ref, spread_ref, out_ref):
    arrived = x_ref[...]
    mixed = jnp.dot(rows_ref[...], arrived, preferred_element_type=jnp.float32)
    extra = arrived[:, 768:896]
    lanes = lanes_ref[...]
    for piece in range(7):
        width = 128 if piece < 6 else 64
        rest = mixed[:, piece * 128 : piece * 128 + 128]
        rotated = None
        for _ in range(3):
            part = rest.astype(jnp.bfloat16)
            rest = rest - part.astype(jnp.float32)
            term = jnp.dot(part, lanes, preferred_element_type=jnp.float32)
            rotated = term if rotated is None else rotated + term
        scale, inverse, level = (
            jnp.dot(
                extra,
                spread_ref[kind, :, piece * 128 : piece * 128 + 128],
                preferred_element_type=jnp.float32,
            )
            for kind in range(3)
        )
        scaled = rotated * (1.0 / 64.0) * inverse
        clipped = jnp.maximum(jnp.minimum(scaled, level), -level)
        quantized = (soft_round(clipped) * scale).astype(jnp.bfloat16)
        out_ref[:, piece * 128 : piece * 128 + width] = quantized[:, :width]


def rotate_and_quantize(arrived):
    rows = np.kron(walsh(64), np.eye(2, dtype=np.float32))
    lanes = np.kron(np.eye(2, dtype=np.float32), walsh(64))
    spread = np.zeros((3, 128, WIDTH), np.float32)
    for kind in range(3):
        for group in range(13):
            spread[kind, 64 + 13 * kind + group, 64 * group : 64 * group + 64] = 1.0
    return pl.pallas_call(
        rotate_kernel,
        out_shape=jax.ShapeDtypeStruct((128, 832), jnp.bfloat16),
        in_specs=[pl.BlockSpec(memory_space=pltpu.VMEM)] * 4,
        out_specs=pl.BlockSpec(memory_space=pltpu.VMEM),
        compiler_params=pltpu.CompilerParams(vmem_limit_bytes=24 * 1024 * 1024),
        cost_estimate=pl.CostEstimate(flops=400_000_000, bytes_accessed=1_500_000, transcendentals=0),
    )(
        arrived,
        jnp.asarray(rows, jnp.bfloat16),
        jnp.asarray(lanes, jnp.bfloat16),
        jnp.asarray(spread, jnp.bfloat16),
    )


def quantize_weight(weight_matrix, weight_exponent):
    scaling = jnp.exp2(weight_exponent.astype(jnp.float32)).astype(jnp.bfloat16).astype(jnp.float32)[None, :]
    clipped = jnp.clip(weight_matrix.astype(jnp.float32) / scaling, -7.5, 7.5)
    return (soft_round(clipped) * scaling).astype(jnp.bfloat16)


def ring(size, shift):
    return [(at, (at + shift) % size) for at in range(size)]


def final_pairs(which):
    pairs = []
    for x in range(4):
        for slot in range(4):
            for y in range(8):
                for c in range(2):
                    first = 3 * (2 * y + c)
                    if which == "main":
                        k = (first + 1) // 16
                    elif first // 16 != (first + 1) // 16:
                        k = first // 16
                    elif (first + 2) // 16 != (first + 1) // 16:
                        k = (first + 2) // 16
                    else:
                        continue
                    owner_l = (4 * ((k - x) % 3) + x) // 3
                    owner_x = (x + SLOTS[slot]) % 4
                    source = ((x * 4 + slot) * 8 + y) * 2 + c
                    pairs.append((source, ((owner_x * 4 + owner_l) * 8 + y) * 2 + c))
    return pairs


def row_order(h, x, y_low, c):
    at = lax.broadcasted_iota(jnp.int32, (384, 384), 0)
    source = lax.broadcasted_iota(jnp.int32, (384, 384), 1)
    core = jnp.where(at < 192, 1 - c, c)
    rest = at % 192
    parity = jnp.where(rest < 96, 1 - y_low, y_low)
    rest = rest % 96
    y = 2 * (rest // 24) + parity
    row = (2 * y + core) * 24 + rest % 24
    shifted = (row - 128 * ((h + x) % 3) + 384) % 384
    return (source == shifted).astype(jnp.bfloat16)


def shards(hidden, down_weight, act_exponent, clip_index, weight_exponent):
    h, x, y_low, c = (lax.axis_index(name) for name in ("h", "x", "yl", "c"))
    y_high = lax.axis_index("yh")

    weight_0 = quantize_weight(down_weight, weight_exponent)
    weight_1 = lax.ppermute(weight_0, "x", ring(4, -1))
    weight_3 = lax.ppermute(weight_0, "x", ring(4, 1))
    weight_2 = jnp.concatenate(
        [
            lax.ppermute(weight_3[:416], "x", ring(4, 1)),
            lax.ppermute(weight_1[416:], "x", ring(4, -1)),
        ],
        axis=0,
    )

    scaling = jnp.exp2(act_exponent.astype(jnp.float32)).astype(jnp.bfloat16)
    inverse = (1.0 / scaling.astype(jnp.float32)).astype(jnp.bfloat16)
    level = jnp.broadcast_to((7.5 - clip_index.astype(jnp.float32)).astype(jnp.bfloat16)[None, :], (128, 13))
    packed = jnp.concatenate([hidden, scaling, inverse, level, jnp.zeros((128, 25), jnp.bfloat16)], axis=1)
    arrived = lax.all_to_all(packed.reshape(64, 2, WIDTH), TENSOR, split_axis=0, concat_axis=0, tiled=True)
    quantized = rotate_and_quantize(arrived.reshape(128, WIDTH))
    returned = lax.all_to_all(quantized.reshape(64, 2, 832), TENSOR, split_axis=0, concat_axis=0, tiled=True)
    own = returned.reshape(128, 832)
    next_1 = lax.ppermute(own, "h", ring(3, -1))
    next_2 = lax.ppermute(own, "h", ring(3, 1))
    gathered = jnp.concatenate([own, next_1, next_2], axis=0)
    acts = jnp.dot(row_order(h, x, y_low, c), gathered, preferred_element_type=jnp.float32).astype(jnp.bfloat16)

    y_pairs_near = [(y, y ^ 1) for y in range(8)]
    y_pairs_far = [(y, (y - 1) % 8 if y % 2 == 0 else (y + 1) % 8) for y in range(8)]
    parts = []
    for weights, y_pairs in (((weight_0, weight_1), y_pairs_near), ((weight_3, weight_2), y_pairs_far)):
        products = [jnp.dot(acts, weight, preferred_element_type=jnp.float32) for weight in weights]
        other = jnp.stack([product[:192] for product in products]).astype(jnp.bfloat16)
        from_core = lax.ppermute(other, "c", [(0, 1), (1, 0)])
        mine = jnp.stack([product[192:] for product in products]) + from_core.astype(jnp.float32)
        from_y = lax.ppermute(mine[:, :96].astype(jnp.bfloat16), ("yh", "yl"), y_pairs)
        parts.append((mine[:, 96:] + from_y.astype(jnp.float32)).astype(jnp.bfloat16))
    sums = jnp.concatenate(parts, axis=0).reshape(16, 24, 1024)
    crossed = lax.all_to_all(sums, ("l", "yh"), split_axis=0, concat_axis=0, tiled=True)
    total = jnp.sum(crossed.astype(jnp.float32), axis=0).astype(jnp.bfloat16)

    y = 2 * y_high + y_low
    early = jnp.logical_and(y == 2, c == 1)
    late = jnp.logical_and(y == 5, c == 0)
    moved = lax.ppermute(total, ("x", "l", "yh", "yl", "c"), final_pairs("main"))
    fixed = lax.ppermute(
        jnp.where(early, total[:8], total[16:]), ("x", "l", "yh", "yl", "c"), final_pairs("fix")
    )
    return jnp.concatenate(
        [jnp.where(early, fixed, moved[:8]), moved[8:16], jnp.where(late, fixed, moved[16:])], axis=0
    )


def solution(mesh):
    fine = Mesh(mesh.devices.reshape(SIZES), AXES)
    rows, columns = ("h", "x"), TENSOR
    placed = (P(rows, columns), P(columns, rows), P(rows, columns), P(columns), P(rows))
    return jax.shard_map(
        shards, mesh=fine, in_specs=placed, out_specs=P(columns, rows), check_vma=False
    )
```

```python
import math

import jax
import jax.numpy as jnp
import numpy as np
from jax import lax
from jax.experimental import pallas as pl
from jax.experimental.pallas import tpu as pltpu
from jax.sharding import Mesh, PartitionSpec as P

AXES = ("h", "x", "l", "yh", "yl", "c")
SIZES = (3, 4, 4, 4, 2, 2)
TENSOR = ("l", "yh", "yl", "c")
SLOTS = (0, 1, 3, 2)
WIDTH = 896
SPLIT = 416


def sine_coefficients():
    nodes = 0.25 * (1.0 + np.cos(np.pi * (np.arange(400) + 0.5) / 400)) ** 1.0
    squares = nodes**2
    target = np.sin(2.0 * np.pi * nodes) / (2.0 * np.pi)
    table = np.stack([nodes * squares**power for power in range(8)], axis=1)
    solved = np.linalg.lstsq(table, target, rcond=None)[0]
    return [float(entry) for entry in solved]


SINE = sine_coefficients()


def soft_round(values):
    rest = values - jnp.round(values)
    squares = rest * rest
    total = jnp.full_like(rest, SINE[-1])
    for entry in SINE[-2::-1]:
        total = total * squares + entry
    return values - rest * total


def walsh(order):
    indices = np.arange(order)
    shared = indices[:, None] & indices[None, :]
    parity = np.zeros((order, order), np.int64)
    for bit_level in range(order.bit_length() - 1):
        parity ^= shared >> bit_level & 1
    return (1 - 2 * parity).astype(np.float32)


def rotate_kernel(x_ref, rows_ref, lanes_ref, spread_ref, out_ref):
    arrived = x_ref[...]
    mixed = jnp.dot(rows_ref[...], arrived, preferred_element_type=jnp.float32)
    extra = arrived[:, 768:896]
    lanes = lanes_ref[...]
    for piece in range(7):
        width = 128 if piece < 6 else 64
        rest = mixed[:, piece * 128 : piece * 128 + 128]
        rotated = None
        for _ in range(3):
            part = rest.astype(jnp.bfloat16)
            rest = rest - part.astype(jnp.float32)
            term = jnp.dot(part, lanes, preferred_element_type=jnp.float32)
            rotated = term if rotated is None else rotated + term
        scale, inverse, level = (
            jnp.dot(
                extra,
                spread_ref[kind, :, piece * 128 : piece * 128 + 128],
                preferred_element_type=jnp.float32,
            )
            for kind in range(3)
        )
        scaled = rotated * (1.0 / 64.0) * inverse
        clipped = jnp.maximum(jnp.minimum(scaled, level), -level)
        quantized = (soft_round(clipped) * scale).astype(jnp.bfloat16)
        out_ref[:, piece * 128 : piece * 128 + width] = quantized[:, :width]


def rotate_and_quantize(arrived):
    rows = np.kron(walsh(64), np.eye(2, dtype=np.float32))
    lanes = np.kron(np.eye(2, dtype=np.float32), walsh(64))
    spread = np.zeros((3, 128, WIDTH), np.float32)
    for kind in range(3):
        for group in range(13):
            spread[kind, 64 + 13 * kind + group, 64 * group : 64 * group + 64] = 1.0
    return pl.pallas_call(
        rotate_kernel,
        out_shape=jax.ShapeDtypeStruct((128, 832), jnp.bfloat16),
        in_specs=[pl.BlockSpec(memory_space=pltpu.VMEM)] * 4,
        out_specs=pl.BlockSpec(memory_space=pltpu.VMEM),
        compiler_params=pltpu.CompilerParams(vmem_limit_bytes=24 * 1024 * 1024),
        cost_estimate=pl.CostEstimate(flops=400_000_000, bytes_accessed=1_500_000, transcendentals=0),
    )(
        arrived,
        jnp.asarray(rows, jnp.bfloat16),
        jnp.asarray(lanes, jnp.bfloat16),
        jnp.asarray(spread, jnp.bfloat16),
    )


def quantize_weight(weight_matrix, weight_exponent):
    scaling = jnp.exp2(weight_exponent.astype(jnp.float32)).astype(jnp.bfloat16).astype(jnp.float32)[None, :]
    clipped = jnp.clip(weight_matrix.astype(jnp.float32) / scaling, -7.5, 7.5)
    return (soft_round(clipped) * scaling).astype(jnp.bfloat16)


def ring(size, shift):
    return [(at, (at + shift) % size) for at in range(size)]


def final_pairs(which):
    pairs = []
    for x in range(4):
        for slot in range(4):
            for y in range(8):
                for c in range(2):
                    first = 3 * (2 * y + c)
                    if which == "main":
                        k = (first + 1) // 16
                    elif first // 16 != (first + 1) // 16:
                        k = first // 16
                    elif (first + 2) // 16 != (first + 1) // 16:
                        k = (first + 2) // 16
                    else:
                        continue
                    owner_l = (4 * ((k - x) % 3) + x) // 3
                    owner_x = (x + SLOTS[slot]) % 4
                    source = ((x * 4 + slot) * 8 + y) * 2 + c
                    pairs.append((source, ((owner_x * 4 + owner_l) * 8 + y) * 2 + c))
    return pairs


def row_order(h, x, y_low, c):
    at = lax.broadcasted_iota(jnp.int32, (384, 384), 0)
    source = lax.broadcasted_iota(jnp.int32, (384, 384), 1)
    core = jnp.where(at < 192, 1 - c, c)
    rest = at % 192
    parity = jnp.where(rest < 96, 1 - y_low, y_low)
    rest = rest % 96
    y = 2 * (rest // 24) + parity
    row = (2 * y + core) * 24 + rest % 24
    shifted = (row - 128 * ((h + x) % 3) + 384) % 384
    return (source == shifted).astype(jnp.bfloat16)


def shards(hidden, down_weight, act_exponent, clip_index, weight_exponent):
    h, x, y_low, c = (lax.axis_index(name) for name in ("h", "x", "yl", "c"))
    y_high = lax.axis_index("yh")

    top_0 = quantize_weight(down_weight[:SPLIT], weight_exponent)
    top_1 = lax.ppermute(top_0, "x", ring(4, -1))
    top_3 = lax.ppermute(top_0, "x", ring(4, 1))
    low_0 = quantize_weight(down_weight[SPLIT:], weight_exponent)

    scaling = jnp.exp2(act_exponent.astype(jnp.float32)).astype(jnp.bfloat16)
    inverse = (1.0 / scaling.astype(jnp.float32)).astype(jnp.bfloat16)
    level = jnp.broadcast_to((7.5 - clip_index.astype(jnp.float32)).astype(jnp.bfloat16)[None, :], (128, 13))
    packed = jnp.concatenate([hidden, scaling, inverse, level, jnp.zeros((128, 25), jnp.bfloat16)], axis=1)
    arrived = lax.all_to_all(packed.reshape(64, 2, WIDTH), TENSOR, split_axis=0, concat_axis=0, tiled=True)
    arrived, top_1, top_3, low_0 = lax.optimization_barrier((arrived, top_1, top_3, low_0))
    low_1 = lax.ppermute(low_0, "x", ring(4, -1))
    low_3 = lax.ppermute(low_0, "x", ring(4, 1))
    quantized = rotate_and_quantize(arrived.reshape(128, WIDTH))
    returned = lax.all_to_all(quantized.reshape(64, 2, 832), TENSOR, split_axis=0, concat_axis=0, tiled=True)
    returned, low_1, low_3 = lax.optimization_barrier((returned, low_1, low_3))
    top_2 = lax.ppermute(top_3, "x", ring(4, 1))
    low_2 = lax.ppermute(low_1, "x", ring(4, -1))
    weight_0, weight_1, weight_2, weight_3 = (
        jnp.concatenate(pair, axis=0)
        for pair in ((top_0, low_0), (top_1, low_1), (top_2, low_2), (top_3, low_3))
    )
    own = returned.reshape(128, 832)
    next_1 = lax.ppermute(own, "h", ring(3, -1))
    next_2 = lax.ppermute(own, "h", ring(3, 1))
    gathered = jnp.concatenate([own, next_1, next_2], axis=0)
    acts = jnp.dot(row_order(h, x, y_low, c), gathered, preferred_element_type=jnp.float32).astype(jnp.bfloat16)

    y_pairs_near = [(y, y ^ 1) for y in range(8)]
    y_pairs_far = [(y, (y - 1) % 8 if y % 2 == 0 else (y + 1) % 8) for y in range(8)]
    parts = []
    for weights, y_pairs in (((weight_0, weight_1), y_pairs_near), ((weight_3, weight_2), y_pairs_far)):
        products = [jnp.dot(acts, weight, preferred_element_type=jnp.float32) for weight in weights]
        other = jnp.stack([product[:192] for product in products]).astype(jnp.bfloat16)
        from_core = lax.ppermute(other, "c", [(0, 1), (1, 0)])
        mine = jnp.stack([product[192:] for product in products]) + from_core.astype(jnp.float32)
        from_y = lax.ppermute(mine[:, :96].astype(jnp.bfloat16), ("yh", "yl"), y_pairs)
        parts.append((mine[:, 96:] + from_y.astype(jnp.float32)).astype(jnp.bfloat16))
    sums = jnp.concatenate(parts, axis=0).reshape(16, 24, 1024)
    crossed = lax.all_to_all(sums, ("l", "yh"), split_axis=0, concat_axis=0, tiled=True)
    total = jnp.sum(crossed.astype(jnp.float32), axis=0).astype(jnp.bfloat16)

    y = 2 * y_high + y_low
    early = jnp.logical_and(y == 2, c == 1)
    late = jnp.logical_and(y == 5, c == 0)
    moved = lax.ppermute(total, ("x", "l", "yh", "yl", "c"), final_pairs("main"))
    fixed = lax.ppermute(
        jnp.where(early, total[:8], total[16:]), ("x", "l", "yh", "yl", "c"), final_pairs("fix")
    )
    return jnp.concatenate(
        [jnp.where(early, fixed, moved[:8]), moved[8:16], jnp.where(late, fixed, moved[16:])], axis=0
    )


def solution(mesh):
    fine = Mesh(mesh.devices.reshape(SIZES), AXES)
    rows, columns = ("h", "x"), TENSOR
    placed = (P(rows, columns), P(columns, rows), P(rows, columns), P(columns), P(rows))
    return jax.shard_map(
        shards, mesh=fine, in_specs=placed, out_specs=P(columns, rows), check_vma=False
    )
```

```python
import math

import jax
import jax.numpy as jnp
import numpy as np
from jax import lax
from jax.experimental import pallas as pl
from jax.experimental.pallas import tpu as pltpu
from jax.sharding import Mesh, PartitionSpec as P

AXES = ("h", "x", "l", "yh", "yl", "c")
SIZES = (3, 4, 4, 4, 2, 2)
TENSOR = ("l", "yh", "yl", "c")
SLOTS = (0, 1, 3, 2)
WIDTH = 896


def sine_coefficients():
    nodes = 0.25 * (1.0 + np.cos(np.pi * (np.arange(400) + 0.5) / 400)) ** 1.0
    squares = nodes**2
    target = np.sin(2.0 * np.pi * nodes) / (2.0 * np.pi)
    table = np.stack([nodes * squares**power for power in range(8)], axis=1)
    solved = np.linalg.lstsq(table, target, rcond=None)[0]
    return [float(entry) for entry in solved]


SINE = sine_coefficients()


def soft_round(values):
    rest = values - jnp.round(values)
    squares = rest * rest
    total = jnp.full_like(rest, SINE[-1])
    for entry in SINE[-2::-1]:
        total = total * squares + entry
    return values - rest * total


def walsh(order):
    indices = np.arange(order)
    shared = indices[:, None] & indices[None, :]
    parity = np.zeros((order, order), np.int64)
    for bit_level in range(order.bit_length() - 1):
        parity ^= shared >> bit_level & 1
    return (1 - 2 * parity).astype(np.float32)


def rotate_kernel(x_ref, rows_ref, lanes_ref, spread_ref, out_ref):
    arrived = x_ref[...]
    mixed = jnp.dot(rows_ref[...], arrived, preferred_element_type=jnp.float32)
    extra = arrived[:, 768:896]
    lanes = lanes_ref[...]
    for piece in range(7):
        width = 128 if piece < 6 else 64
        rest = mixed[:, piece * 128 : piece * 128 + 128]
        rotated = None
        for _ in range(3):
            part = rest.astype(jnp.bfloat16)
            rest = rest - part.astype(jnp.float32)
            term = jnp.dot(part, lanes, preferred_element_type=jnp.float32)
            rotated = term if rotated is None else rotated + term
        scale, inverse, level = (
            jnp.dot(
                extra,
                spread_ref[kind, :, piece * 128 : piece * 128 + 128],
                preferred_element_type=jnp.float32,
            )
            for kind in range(3)
        )
        scaled = rotated * (1.0 / 64.0) * inverse
        clipped = jnp.maximum(jnp.minimum(scaled, level), -level)
        quantized = (soft_round(clipped) * scale).astype(jnp.bfloat16)
        out_ref[:, piece * 128 : piece * 128 + width] = quantized[:, :width]


def rotate_and_quantize(arrived):
    rows = np.kron(walsh(64), np.eye(2, dtype=np.float32))
    lanes = np.kron(np.eye(2, dtype=np.float32), walsh(64))
    spread = np.zeros((3, 128, WIDTH), np.float32)
    for kind in range(3):
        for group in range(13):
            spread[kind, 64 + 13 * kind + group, 64 * group : 64 * group + 64] = 1.0
    return pl.pallas_call(
        rotate_kernel,
        out_shape=jax.ShapeDtypeStruct((128, 832), jnp.bfloat16),
        in_specs=[pl.BlockSpec(memory_space=pltpu.VMEM)] * 4,
        out_specs=pl.BlockSpec(memory_space=pltpu.VMEM),
        compiler_params=pltpu.CompilerParams(vmem_limit_bytes=24 * 1024 * 1024),
        cost_estimate=pl.CostEstimate(flops=400_000_000, bytes_accessed=1_500_000, transcendentals=0),
    )(
        arrived,
        jnp.asarray(rows, jnp.bfloat16),
        jnp.asarray(lanes, jnp.bfloat16),
        jnp.asarray(spread, jnp.bfloat16),
    )


def pack_kernel(hidden_ref, exponent_ref, index_ref, place_ref, out_ref):
    out_ref[:, :768] = hidden_ref[:, :768]
    scaling = jnp.exp2(exponent_ref[...].astype(jnp.float32)).astype(jnp.bfloat16)
    inverse = (1.0 / scaling.astype(jnp.float32)).astype(jnp.bfloat16)
    level = jnp.broadcast_to(7.5 - index_ref[...].astype(jnp.float32), (128, 13)).astype(jnp.bfloat16)
    tail = jnp.dot(hidden_ref[:, 768:], place_ref[:64], preferred_element_type=jnp.float32)
    for kind, extra in enumerate((scaling, inverse, level)):
        tail += jnp.dot(extra, place_ref[64 + 16 * kind : 77 + 16 * kind], preferred_element_type=jnp.float32)
    out_ref[:, 768:] = tail.astype(jnp.bfloat16)


def pack(hidden, act_exponent, clip_index):
    place = np.zeros((112, 128), np.float32)
    place[np.arange(64), np.arange(64)] = 1.0
    for kind in range(3):
        place[64 + 16 * kind + np.arange(13), 64 + 13 * kind + np.arange(13)] = 1.0
    return pl.pallas_call(
        pack_kernel,
        out_shape=jax.ShapeDtypeStruct((128, WIDTH), jnp.bfloat16),
        in_specs=[pl.BlockSpec(memory_space=pltpu.VMEM)] * 4,
        out_specs=pl.BlockSpec(memory_space=pltpu.VMEM),
        compiler_params=pltpu.CompilerParams(vmem_limit_bytes=16 * 1024 * 1024),
        cost_estimate=pl.CostEstimate(flops=4_000_000, bytes_accessed=500_000, transcendentals=0),
    )(hidden, act_exponent, clip_index.reshape(1, 13), jnp.asarray(place, jnp.bfloat16))


def accumulate(acts, pieces):
    total, start = None, 0
    for piece in pieces:
        stop = start + piece.shape[0]
        term = jnp.dot(acts[:, start:stop], piece[...], preferred_element_type=jnp.float32)
        total = term if total is None else total + term
        start = stop
    return total


def product_kernel(counts, acts_ref, *refs):
    *pieces, other_ref, mine_ref = refs
    start = 0
    acts = acts_ref[...]
    for at, count in enumerate(counts):
        product = accumulate(acts, pieces[start : start + count])
        other_ref[at] = product[:192].astype(jnp.bfloat16)
        mine_ref[at] = product[192:]
        start += count


def products(acts, weights):
    flat = [piece for weight in weights for piece in weight]
    counts = tuple(len(weight) for weight in weights)
    return pl.pallas_call(
        lambda *refs: product_kernel(counts, *refs),
        out_shape=(
            jax.ShapeDtypeStruct((2, 192, 1024), jnp.bfloat16),
            jax.ShapeDtypeStruct((2, 192, 1024), jnp.float32),
        ),
        in_specs=[pl.BlockSpec(memory_space=pltpu.VMEM)] * (1 + len(flat)),
        out_specs=(pl.BlockSpec(memory_space=pltpu.VMEM),) * 2,
        compiler_params=pltpu.CompilerParams(vmem_limit_bytes=32 * 1024 * 1024),
        cost_estimate=pl.CostEstimate(flops=1_300_000_000, bytes_accessed=6_000_000, transcendentals=0),
    )(acts, *flat)


def arrange_kernel(source_ref, own_ref, next_1_ref, next_2_ref, out_ref):
    column = lax.broadcasted_iota(jnp.int32, (384, 128), 1)
    source = source_ref[...]
    total = None
    for at, rows_ref in enumerate((own_ref, next_1_ref, next_2_ref)):
        chosen = jnp.where(source == column + 128 * at, 1.0, 0.0).astype(jnp.bfloat16)
        term = jnp.dot(chosen, rows_ref[...], preferred_element_type=jnp.float32)
        total = term if total is None else total + term
    out_ref[...] = total.astype(jnp.bfloat16)


def arrange(source, own, next_1, next_2):
    return pl.pallas_call(
        arrange_kernel,
        out_shape=jax.ShapeDtypeStruct((384, 832), jnp.bfloat16),
        in_specs=[pl.BlockSpec(memory_space=pltpu.VMEM)] * 4,
        out_specs=pl.BlockSpec(memory_space=pltpu.VMEM),
        compiler_params=pltpu.CompilerParams(vmem_limit_bytes=16 * 1024 * 1024),
        cost_estimate=pl.CostEstimate(flops=20_000_000_000, bytes_accessed=1_500_000, transcendentals=0),
    )(source, own, next_1, next_2)


def quantize_weight(weight_matrix, weight_exponent):
    scaling = jnp.exp2(weight_exponent.astype(jnp.float32)).astype(jnp.bfloat16).astype(jnp.float32)[None, :]
    clipped = jnp.clip(weight_matrix.astype(jnp.float32) / scaling, -7.5, 7.5)
    return (soft_round(clipped) * scaling).astype(jnp.bfloat16)


def ring(size, shift):
    return [(at, (at + shift) % size) for at in range(size)]


def final_pairs(which):
    pairs = []
    for x in range(4):
        for slot in range(4):
            for y in range(8):
                for c in range(2):
                    first = 3 * (2 * y + c)
                    if which == "main":
                        k = (first + 1) // 16
                    elif first // 16 != (first + 1) // 16:
                        k = first // 16
                    elif (first + 2) // 16 != (first + 1) // 16:
                        k = (first + 2) // 16
                    else:
                        continue
                    owner_l = (4 * ((k - x) % 3) + x) // 3
                    owner_x = (x + SLOTS[slot]) % 4
                    source = ((x * 4 + slot) * 8 + y) * 2 + c
                    pairs.append((source, ((owner_x * 4 + owner_l) * 8 + y) * 2 + c))
    return pairs


def row_order(h, x, y_low, c):
    at = lax.broadcasted_iota(jnp.int32, (384, 1), 0)
    core = jnp.where(at < 192, 1 - c, c)
    rest = at % 192
    parity = jnp.where(rest < 96, 1 - y_low, y_low)
    rest = rest % 96
    y = 2 * (rest // 24) + parity
    row = (2 * y + core) * 24 + rest % 24
    return (row - 128 * ((h + x) % 3) + 384) % 384


def shards(hidden, down_weight, act_exponent, clip_index, weight_exponent):
    h, x, y_low, c = (lax.axis_index(name) for name in ("h", "x", "yl", "c"))
    y_high = lax.axis_index("yh")

    def quantized_rows(source, start, stop):
        return quantize_weight(source[start:stop], weight_exponent)

    def to_right(rows):
        return lax.ppermute(rows, "x", ring(4, 1))

    def to_left(rows):
        return lax.ppermute(rows, "x", ring(4, -1))

    packed = pack(hidden, act_exponent, clip_index)
    arrived = lax.all_to_all(packed.reshape(64, 2, WIDTH), TENSOR, split_axis=0, concat_axis=0, tiled=True)
    first_0 = quantized_rows(down_weight, 0, 256)
    third_0 = quantized_rows(down_weight, 512, 832)
    first_3, third_1 = to_right(first_0), to_left(third_0)

    quantized = rotate_and_quantize(arrived.reshape(128, WIDTH))
    returned = lax.all_to_all(quantized.reshape(64, 2, 832), TENSOR, split_axis=0, concat_axis=0, tiled=True)
    second_3 = to_right(quantized_rows(down_weight, 256, 640))
    second_1 = to_left(quantized_rows(down_weight, 128, 512))
    second_0 = quantized_rows(down_weight, 256, 512)

    own = returned.reshape(128, 832)
    next_1 = lax.ppermute(own, "h", ring(3, -1))
    next_2 = lax.ppermute(own, "h", ring(3, 1))
    last_3 = to_right(third_0[128:])
    last_1 = to_left(first_0[:128])
    early_2 = to_right(jnp.concatenate([first_3, second_3[:128]], axis=0))
    late_2 = to_left(jnp.concatenate([second_1[256:], third_1], axis=0))
    weight_0 = (first_0, second_0, third_0)
    weight_1 = (last_1, second_1, third_1)
    weight_2 = (early_2, late_2)
    weight_3 = (first_3, second_3, last_3)
    acts = arrange(row_order(h, x, y_low, c), own, next_1, next_2)

    y_pairs_near = [(y, y ^ 1) for y in range(8)]
    y_pairs_far = [(y, (y - 1) % 8 if y % 2 == 0 else (y + 1) % 8) for y in range(8)]
    parts = []
    for weights, y_pairs in (((weight_0, weight_1), y_pairs_near), ((weight_3, weight_2), y_pairs_far)):
        other, own_rows = products(acts, weights)
        from_core = lax.ppermute(other, "c", [(0, 1), (1, 0)])
        mine = own_rows + from_core.astype(jnp.float32)
        from_y = lax.ppermute(mine[:, :96].astype(jnp.bfloat16), ("yh", "yl"), y_pairs)
        parts.append((mine[:, 96:] + from_y.astype(jnp.float32)).astype(jnp.bfloat16))
    sums = jnp.concatenate(parts, axis=0).reshape(16, 24, 1024)
    crossed = lax.all_to_all(sums, ("l", "yh"), split_axis=0, concat_axis=0, tiled=True)
    total = jnp.sum(crossed.astype(jnp.float32), axis=0).astype(jnp.bfloat16)

    y = 2 * y_high + y_low
    early = jnp.logical_and(y == 2, c == 1)
    late = jnp.logical_and(y == 5, c == 0)
    moved = lax.ppermute(total, ("x", "l", "yh", "yl", "c"), final_pairs("main"))
    fixed = lax.ppermute(
        jnp.where(early, total[:8], total[16:]), ("x", "l", "yh", "yl", "c"), final_pairs("fix")
    )
    return jnp.concatenate(
        [jnp.where(early, fixed, moved[:8]), moved[8:16], jnp.where(late, fixed, moved[16:])], axis=0
    )


def solution(mesh):
    fine = Mesh(mesh.devices.reshape(SIZES), AXES)
    rows, columns = ("h", "x"), TENSOR
    placed = (P(rows, columns), P(columns, rows), P(rows, columns), P(columns), P(rows))
    return jax.shard_map(
        shards, mesh=fine, in_specs=placed, out_specs=P(columns, rows), check_vma=False
    )
```

```python
import math

import jax
import jax.numpy as jnp
import numpy as np
from jax import lax
from jax.experimental import pallas as pl
from jax.experimental.pallas import tpu as pltpu
from jax.sharding import Mesh, PartitionSpec as P

AXES = ("h", "x", "l", "yh", "yl", "c")
SIZES = (3, 4, 4, 4, 2, 2)
TENSOR = ("l", "yh", "yl", "c")
SLOTS = (0, 1, 3, 2)
WIDTH = 896
SPLIT = 384


def sine_coefficients():
    nodes = 0.25 * (1.0 + np.cos(np.pi * (np.arange(400) + 0.5) / 400)) ** 1.0
    squares = nodes**2
    target = np.sin(2.0 * np.pi * nodes) / (2.0 * np.pi)
    table = np.stack([nodes * squares**power for power in range(8)], axis=1)
    solved = np.linalg.lstsq(table, target, rcond=None)[0]
    return [float(entry) for entry in solved]


SINE = sine_coefficients()


def soft_round(values):
    rest = values - jnp.round(values)
    squares = rest * rest
    total = jnp.full_like(rest, SINE[-1])
    for entry in SINE[-2::-1]:
        total = total * squares + entry
    return values - rest * total


def walsh(order):
    indices = np.arange(order)
    shared = indices[:, None] & indices[None, :]
    parity = np.zeros((order, order), np.int64)
    for bit_level in range(order.bit_length() - 1):
        parity ^= shared >> bit_level & 1
    return (1 - 2 * parity).astype(np.float32)


def rotate_kernel(x_ref, rows_ref, lanes_ref, spread_ref, out_ref):
    arrived = x_ref[...]
    mixed = jnp.dot(rows_ref[...], arrived, preferred_element_type=jnp.float32)
    extra = arrived[:, 768:896]
    lanes = lanes_ref[...]
    for piece in range(7):
        width = 128 if piece < 6 else 64
        rest = mixed[:, piece * 128 : piece * 128 + 128]
        rotated = None
        for _ in range(3):
            part = rest.astype(jnp.bfloat16)
            rest = rest - part.astype(jnp.float32)
            term = jnp.dot(part, lanes, preferred_element_type=jnp.float32)
            rotated = term if rotated is None else rotated + term
        scale, inverse, level = (
            jnp.dot(
                extra,
                spread_ref[kind, :, piece * 128 : piece * 128 + 128],
                preferred_element_type=jnp.float32,
            )
            for kind in range(3)
        )
        scaled = rotated * (1.0 / 64.0) * inverse
        clipped = jnp.maximum(jnp.minimum(scaled, level), -level)
        quantized = (soft_round(clipped) * scale).astype(jnp.bfloat16)
        out_ref[:, piece * 128 : piece * 128 + width] = quantized[:, :width]


def rotate_and_quantize(arrived):
    rows = np.kron(walsh(64), np.eye(2, dtype=np.float32))
    lanes = np.kron(np.eye(2, dtype=np.float32), walsh(64))
    spread = np.zeros((3, 128, WIDTH), np.float32)
    for kind in range(3):
        for group in range(13):
            spread[kind, 64 + 13 * kind + group, 64 * group : 64 * group + 64] = 1.0
    return pl.pallas_call(
        rotate_kernel,
        out_shape=jax.ShapeDtypeStruct((128, 832), jnp.bfloat16),
        in_specs=[pl.BlockSpec(memory_space=pltpu.VMEM)] * 4,
        out_specs=pl.BlockSpec(memory_space=pltpu.VMEM),
        compiler_params=pltpu.CompilerParams(vmem_limit_bytes=24 * 1024 * 1024),
        cost_estimate=pl.CostEstimate(flops=400_000_000, bytes_accessed=1_500_000, transcendentals=0),
    )(
        arrived,
        jnp.asarray(rows, jnp.bfloat16),
        jnp.asarray(lanes, jnp.bfloat16),
        jnp.asarray(spread, jnp.bfloat16),
    )


def accumulate(acts, pieces):
    total, start = None, 0
    for piece in pieces:
        stop = start + piece.shape[0]
        term = jnp.dot(acts[:, start:stop], piece[...], preferred_element_type=jnp.float32)
        total = term if total is None else total + term
        start = stop
    return total


def product_kernel(counts, acts_ref, *refs):
    *pieces, other_ref, mine_ref = refs
    start = 0
    acts = acts_ref[...]
    for at, count in enumerate(counts):
        product = accumulate(acts, pieces[start : start + count])
        other_ref[at] = product[:192].astype(jnp.bfloat16)
        mine_ref[at] = product[192:]
        start += count


def products(acts, weights):
    flat = [piece for weight in weights for piece in weight]
    counts = tuple(len(weight) for weight in weights)
    return pl.pallas_call(
        lambda *refs: product_kernel(counts, *refs),
        out_shape=(
            jax.ShapeDtypeStruct((2, 192, 1024), jnp.bfloat16),
            jax.ShapeDtypeStruct((2, 192, 1024), jnp.float32),
        ),
        in_specs=[pl.BlockSpec(memory_space=pltpu.VMEM)] * (1 + len(flat)),
        out_specs=(pl.BlockSpec(memory_space=pltpu.VMEM),) * 2,
        compiler_params=pltpu.CompilerParams(vmem_limit_bytes=32 * 1024 * 1024),
        cost_estimate=pl.CostEstimate(flops=1_300_000_000, bytes_accessed=6_000_000, transcendentals=0),
    )(acts, *flat)


def arrange_kernel(source_ref, own_ref, next_1_ref, next_2_ref, out_ref):
    column = lax.broadcasted_iota(jnp.int32, (384, 128), 1)
    source = source_ref[...]
    total = None
    for at, rows_ref in enumerate((own_ref, next_1_ref, next_2_ref)):
        chosen = jnp.where(source == column + 128 * at, 1.0, 0.0).astype(jnp.bfloat16)
        term = jnp.dot(chosen, rows_ref[...], preferred_element_type=jnp.float32)
        total = term if total is None else total + term
    out_ref[...] = total.astype(jnp.bfloat16)


def arrange(source, own, next_1, next_2):
    return pl.pallas_call(
        arrange_kernel,
        out_shape=jax.ShapeDtypeStruct((384, 832), jnp.bfloat16),
        in_specs=[pl.BlockSpec(memory_space=pltpu.VMEM)] * 4,
        out_specs=pl.BlockSpec(memory_space=pltpu.VMEM),
        compiler_params=pltpu.CompilerParams(vmem_limit_bytes=16 * 1024 * 1024),
        cost_estimate=pl.CostEstimate(flops=20_000_000_000, bytes_accessed=1_500_000, transcendentals=0),
    )(source, own, next_1, next_2)


def quantize_weight(weight_matrix, weight_exponent):
    scaling = jnp.exp2(weight_exponent.astype(jnp.float32)).astype(jnp.bfloat16).astype(jnp.float32)[None, :]
    clipped = jnp.clip(weight_matrix.astype(jnp.float32) / scaling, -7.5, 7.5)
    return (soft_round(clipped) * scaling).astype(jnp.bfloat16)


def ring(size, shift):
    return [(at, (at + shift) % size) for at in range(size)]


def final_pairs(which):
    pairs = []
    for x in range(4):
        for slot in range(4):
            for y in range(8):
                for c in range(2):
                    first = 3 * (2 * y + c)
                    if which == "main":
                        k = (first + 1) // 16
                    elif first // 16 != (first + 1) // 16:
                        k = first // 16
                    elif (first + 2) // 16 != (first + 1) // 16:
                        k = (first + 2) // 16
                    else:
                        continue
                    owner_l = (4 * ((k - x) % 3) + x) // 3
                    owner_x = (x + SLOTS[slot]) % 4
                    source = ((x * 4 + slot) * 8 + y) * 2 + c
                    pairs.append((source, ((owner_x * 4 + owner_l) * 8 + y) * 2 + c))
    return pairs


def row_order(h, x, y_low, c):
    at = lax.broadcasted_iota(jnp.int32, (384, 1), 0)
    core = jnp.where(at < 192, 1 - c, c)
    rest = at % 192
    parity = jnp.where(rest < 96, 1 - y_low, y_low)
    rest = rest % 96
    y = 2 * (rest // 24) + parity
    row = (2 * y + core) * 24 + rest % 24
    return (row - 128 * ((h + x) % 3) + 384) % 384


def shards(hidden, down_weight, act_exponent, clip_index, weight_exponent):
    h, x, y_low, c = (lax.axis_index(name) for name in ("h", "x", "yl", "c"))
    y_high = lax.axis_index("yh")

    def to_right(rows):
        return lax.ppermute(rows, "x", ring(4, 1))

    def to_left(rows):
        return lax.ppermute(rows, "x", ring(4, -1))

    top_0 = quantize_weight(down_weight[:SPLIT], weight_exponent)
    top_1, top_3 = to_left(top_0), to_right(top_0)
    scaling = jnp.exp2(act_exponent.astype(jnp.float32)).astype(jnp.bfloat16)
    inverse = (1.0 / scaling.astype(jnp.float32)).astype(jnp.bfloat16)
    level = jnp.broadcast_to((7.5 - clip_index.astype(jnp.float32)).astype(jnp.bfloat16)[None, :], (128, 13))
    packed = jnp.concatenate([hidden, scaling, inverse, level, jnp.zeros((128, 25), jnp.bfloat16)], axis=1)
    packed, down_weight = lax.optimization_barrier((packed, down_weight))
    low_0 = quantize_weight(down_weight[SPLIT:], weight_exponent)
    arrived = lax.all_to_all(packed.reshape(64, 2, WIDTH), TENSOR, split_axis=0, concat_axis=0, tiled=True)
    arrived, top_1, top_3 = lax.optimization_barrier((arrived, top_1, top_3))
    quantized = rotate_and_quantize(arrived.reshape(128, WIDTH))
    returned = lax.all_to_all(quantized.reshape(64, 2, 832), TENSOR, split_axis=0, concat_axis=0, tiled=True)
    low_1, low_3 = to_left(low_0), to_right(low_0)
    returned, low_1, low_3 = lax.optimization_barrier((returned, low_1, low_3))
    own = returned.reshape(128, 832)
    next_1 = lax.ppermute(own, "h", ring(3, -1))
    next_2 = lax.ppermute(own, "h", ring(3, 1))
    top_2, low_2 = to_right(top_3), to_left(low_1)
    weight_0, weight_1, weight_2, weight_3 = (top_0, low_0), (top_1, low_1), (top_2, low_2), (top_3, low_3)
    acts = arrange(row_order(h, x, y_low, c), own, next_1, next_2)

    y_pairs_near = [(y, y ^ 1) for y in range(8)]
    y_pairs_far = [(y, (y - 1) % 8 if y % 2 == 0 else (y + 1) % 8) for y in range(8)]
    parts = []
    for weights, y_pairs in (((weight_0, weight_1), y_pairs_near), ((weight_3, weight_2), y_pairs_far)):
        other, own_rows = products(acts, weights)
        from_core = lax.ppermute(other, "c", [(0, 1), (1, 0)])
        mine = own_rows + from_core.astype(jnp.float32)
        from_y = lax.ppermute(mine[:, :96].astype(jnp.bfloat16), ("yh", "yl"), y_pairs)
        parts.append((mine[:, 96:] + from_y.astype(jnp.float32)).astype(jnp.bfloat16))
    sums = jnp.concatenate(parts, axis=0).reshape(16, 24, 1024)
    crossed = lax.all_to_all(sums, ("l", "yh"), split_axis=0, concat_axis=0, tiled=True)
    total = jnp.sum(crossed.astype(jnp.float32), axis=0).astype(jnp.bfloat16)

    y = 2 * y_high + y_low
    early = jnp.logical_and(y == 2, c == 1)
    late = jnp.logical_and(y == 5, c == 0)
    moved = lax.ppermute(total, ("x", "l", "yh", "yl", "c"), final_pairs("main"))
    fixed = lax.ppermute(
        jnp.where(early, total[:8], total[16:]), ("x", "l", "yh", "yl", "c"), final_pairs("fix")
    )
    return jnp.concatenate(
        [jnp.where(early, fixed, moved[:8]), moved[8:16], jnp.where(late, fixed, moved[16:])], axis=0
    )


def solution(mesh):
    fine = Mesh(mesh.devices.reshape(SIZES), AXES)
    rows, columns = ("h", "x"), TENSOR
    placed = (P(rows, columns), P(columns, rows), P(rows, columns), P(columns), P(rows))
    return jax.shard_map(
        shards, mesh=fine, in_specs=placed, out_specs=P(columns, rows), check_vma=False
    )
```

```python
import math

import jax
import jax.numpy as jnp
import numpy as np
from jax import lax
from jax.experimental import pallas as pl
from jax.experimental.pallas import tpu as pltpu
from jax.sharding import Mesh, PartitionSpec as P

AXES = ("h", "x", "l", "yh", "yl", "c")
SIZES = (3, 4, 4, 4, 2, 2)
TENSOR = ("l", "yh", "yl", "c")
SLOTS = (0, 1, 3, 2)
WIDTH = 896
SPLIT = 384


def sine_coefficients():
    nodes = 0.25 * (1.0 + np.cos(np.pi * (np.arange(400) + 0.5) / 400)) ** 1.0
    squares = nodes**2
    target = np.sin(2.0 * np.pi * nodes) / (2.0 * np.pi)
    table = np.stack([nodes * squares**power for power in range(8)], axis=1)
    solved = np.linalg.lstsq(table, target, rcond=None)[0]
    return [float(entry) for entry in solved]


SINE = sine_coefficients()


def soft_round(values):
    rest = values - jnp.round(values)
    squares = rest * rest
    total = jnp.full_like(rest, SINE[-1])
    for entry in SINE[-2::-1]:
        total = total * squares + entry
    return values - rest * total


def walsh(order):
    indices = np.arange(order)
    shared = indices[:, None] & indices[None, :]
    parity = np.zeros((order, order), np.int64)
    for bit_level in range(order.bit_length() - 1):
        parity ^= shared >> bit_level & 1
    return (1 - 2 * parity).astype(np.float32)


def rotate_kernel(x_ref, rows_ref, lanes_ref, spread_ref, out_ref):
    arrived = x_ref[...]
    mixed = jnp.dot(rows_ref[...], arrived, preferred_element_type=jnp.float32)
    extra = arrived[:, 768:896]
    lanes = lanes_ref[...]
    for piece in range(7):
        width = 128 if piece < 6 else 64
        rest = mixed[:, piece * 128 : piece * 128 + 128]
        rotated = None
        for _ in range(3):
            part = rest.astype(jnp.bfloat16)
            rest = rest - part.astype(jnp.float32)
            term = jnp.dot(part, lanes, preferred_element_type=jnp.float32)
            rotated = term if rotated is None else rotated + term
        scale, inverse, level = (
            jnp.dot(
                extra,
                spread_ref[kind, :, piece * 128 : piece * 128 + 128],
                preferred_element_type=jnp.float32,
            )
            for kind in range(3)
        )
        scaled = rotated * (1.0 / 64.0) * inverse
        clipped = jnp.maximum(jnp.minimum(scaled, level), -level)
        quantized = (soft_round(clipped) * scale).astype(jnp.bfloat16)
        out_ref[:, piece * 128 : piece * 128 + width] = quantized[:, :width]


def rotate_and_quantize(arrived):
    rows = np.kron(walsh(64), np.eye(2, dtype=np.float32))
    lanes = np.kron(np.eye(2, dtype=np.float32), walsh(64))
    spread = np.zeros((3, 128, WIDTH), np.float32)
    for kind in range(3):
        for group in range(13):
            spread[kind, 64 + 13 * kind + group, 64 * group : 64 * group + 64] = 1.0
    return pl.pallas_call(
        rotate_kernel,
        out_shape=jax.ShapeDtypeStruct((128, 832), jnp.bfloat16),
        in_specs=[pl.BlockSpec(memory_space=pltpu.VMEM)] * 4,
        out_specs=pl.BlockSpec(memory_space=pltpu.VMEM),
        compiler_params=pltpu.CompilerParams(vmem_limit_bytes=24 * 1024 * 1024),
        cost_estimate=pl.CostEstimate(flops=40000000000, bytes_accessed=1_500_000, transcendentals=0),
    )(
        arrived,
        jnp.asarray(rows, jnp.bfloat16),
        jnp.asarray(lanes, jnp.bfloat16),
        jnp.asarray(spread, jnp.bfloat16),
    )


def accumulate(acts, pieces):
    total, start = None, 0
    for piece in pieces:
        stop = start + piece.shape[0]
        term = jnp.dot(acts[:, start:stop], piece[...], preferred_element_type=jnp.float32)
        total = term if total is None else total + term
        start = stop
    return total


def product_kernel(counts, acts_ref, *refs):
    *pieces, other_ref, mine_ref = refs
    start = 0
    acts = acts_ref[...]
    for at, count in enumerate(counts):
        product = accumulate(acts, pieces[start : start + count])
        other_ref[at] = product[:192].astype(jnp.bfloat16)
        mine_ref[at] = product[192:]
        start += count


def products(acts, weights):
    flat = [piece for weight in weights for piece in weight]
    counts = tuple(len(weight) for weight in weights)
    return pl.pallas_call(
        lambda *refs: product_kernel(counts, *refs),
        out_shape=(
            jax.ShapeDtypeStruct((2, 192, 1024), jnp.bfloat16),
            jax.ShapeDtypeStruct((2, 192, 1024), jnp.float32),
        ),
        in_specs=[pl.BlockSpec(memory_space=pltpu.VMEM)] * (1 + len(flat)),
        out_specs=(pl.BlockSpec(memory_space=pltpu.VMEM),) * 2,
        compiler_params=pltpu.CompilerParams(vmem_limit_bytes=32 * 1024 * 1024),
        cost_estimate=pl.CostEstimate(flops=1_300_000_000, bytes_accessed=6_000_000, transcendentals=0),
    )(acts, *flat)


def arrange_kernel(source_ref, own_ref, next_1_ref, next_2_ref, out_ref):
    column = lax.broadcasted_iota(jnp.int32, (384, 128), 1)
    source = source_ref[...]
    total = None
    for at, rows_ref in enumerate((own_ref, next_1_ref, next_2_ref)):
        chosen = jnp.where(source == column + 128 * at, 1.0, 0.0).astype(jnp.bfloat16)
        term = jnp.dot(chosen, rows_ref[...], preferred_element_type=jnp.float32)
        total = term if total is None else total + term
    out_ref[...] = total.astype(jnp.bfloat16)


def arrange(source, own, next_1, next_2):
    return pl.pallas_call(
        arrange_kernel,
        out_shape=jax.ShapeDtypeStruct((384, 832), jnp.bfloat16),
        in_specs=[pl.BlockSpec(memory_space=pltpu.VMEM)] * 4,
        out_specs=pl.BlockSpec(memory_space=pltpu.VMEM),
        compiler_params=pltpu.CompilerParams(vmem_limit_bytes=16 * 1024 * 1024),
        cost_estimate=pl.CostEstimate(flops=20000000000, bytes_accessed=1_500_000, transcendentals=0),
    )(source, own, next_1, next_2)


def quantize_weight(weight_matrix, weight_exponent):
    scaling = jnp.exp2(weight_exponent.astype(jnp.float32)).astype(jnp.bfloat16).astype(jnp.float32)[None, :]
    clipped = jnp.clip(weight_matrix.astype(jnp.float32) / scaling, -7.5, 7.5)
    return (soft_round(clipped) * scaling).astype(jnp.bfloat16)


def ring(size, shift):
    return [(at, (at + shift) % size) for at in range(size)]


def final_pairs(which):
    pairs = []
    for x in range(4):
        for slot in range(4):
            for y in range(8):
                for c in range(2):
                    first = 3 * (2 * y + c)
                    if which == "main":
                        k = (first + 1) // 16
                    elif first // 16 != (first + 1) // 16:
                        k = first // 16
                    elif (first + 2) // 16 != (first + 1) // 16:
                        k = (first + 2) // 16
                    else:
                        continue
                    owner_l = (4 * ((k - x) % 3) + x) // 3
                    owner_x = (x + SLOTS[slot]) % 4
                    source = ((x * 4 + slot) * 8 + y) * 2 + c
                    pairs.append((source, ((owner_x * 4 + owner_l) * 8 + y) * 2 + c))
    return pairs


def row_order(h, x, y_low, c):
    at = lax.broadcasted_iota(jnp.int32, (384, 1), 0)
    core = jnp.where(at < 192, 1 - c, c)
    rest = at % 192
    parity = jnp.where(rest < 96, 1 - y_low, y_low)
    rest = rest % 96
    y = 2 * (rest // 24) + parity
    row = (2 * y + core) * 24 + rest % 24
    return (row - 128 * ((h + x) % 3) + 384) % 384


def shards(hidden, down_weight, act_exponent, clip_index, weight_exponent):
    h, x, y_low, c = (lax.axis_index(name) for name in ("h", "x", "yl", "c"))
    y_high = lax.axis_index("yh")

    def to_right(rows):
        return lax.ppermute(rows, "x", ring(4, 1))

    def to_left(rows):
        return lax.ppermute(rows, "x", ring(4, -1))

    scaling = jnp.exp2(act_exponent.astype(jnp.float32)).astype(jnp.bfloat16)
    inverse = (1.0 / scaling.astype(jnp.float32)).astype(jnp.bfloat16)
    level = jnp.broadcast_to((7.5 - clip_index.astype(jnp.float32)).astype(jnp.bfloat16)[None, :], (128, 13))
    packed = jnp.concatenate([hidden, scaling, inverse, level, jnp.zeros((128, 25), jnp.bfloat16)], axis=1)
    packed, down_weight = lax.optimization_barrier((packed, down_weight))
    weight_0 = quantize_weight(down_weight, weight_exponent)
    weight_1, weight_3 = to_left(weight_0), to_right(weight_0)
    arrived = lax.all_to_all(packed.reshape(64, 2, WIDTH), TENSOR, split_axis=0, concat_axis=0, tiled=True)
    quantized = rotate_and_quantize(arrived.reshape(128, WIDTH))
    returned = lax.all_to_all(quantized.reshape(64, 2, 832), TENSOR, split_axis=0, concat_axis=0, tiled=True)
    own = returned.reshape(128, 832)
    next_1 = lax.ppermute(own, "h", ring(3, -1))
    next_2 = lax.ppermute(own, "h", ring(3, 1))
    weight_2 = (to_right(weight_3[:SPLIT]), to_left(weight_1[SPLIT:]))
    acts = arrange(row_order(h, x, y_low, c), own, next_1, next_2)

    y_pairs_near = [(y, y ^ 1) for y in range(8)]
    y_pairs_far = [(y, (y - 1) % 8 if y % 2 == 0 else (y + 1) % 8) for y in range(8)]
    parts = []
    for weights, y_pairs in ((((weight_0,), (weight_1,)), y_pairs_near), (((weight_3,), weight_2), y_pairs_far)):
        other, own_rows = products(acts, weights)
        from_core = lax.ppermute(other, "c", [(0, 1), (1, 0)])
        mine = own_rows + from_core.astype(jnp.float32)
        from_y = lax.ppermute(mine[:, :96].astype(jnp.bfloat16), ("yh", "yl"), y_pairs)
        parts.append((mine[:, 96:] + from_y.astype(jnp.float32)).astype(jnp.bfloat16))
    sums = jnp.concatenate(parts, axis=0).reshape(16, 24, 1024)
    crossed = lax.all_to_all(sums, ("l", "yh"), split_axis=0, concat_axis=0, tiled=True)
    total = jnp.sum(crossed.astype(jnp.float32), axis=0).astype(jnp.bfloat16)

    y = 2 * y_high + y_low
    early = jnp.logical_and(y == 2, c == 1)
    late = jnp.logical_and(y == 5, c == 0)
    moved = lax.ppermute(total, ("x", "l", "yh", "yl", "c"), final_pairs("main"))
    fixed = lax.ppermute(
        jnp.where(early, total[:8], total[16:]), ("x", "l", "yh", "yl", "c"), final_pairs("fix")
    )
    return jnp.concatenate(
        [jnp.where(early, fixed, moved[:8]), moved[8:16], jnp.where(late, fixed, moved[16:])], axis=0
    )


def solution(mesh):
    fine = Mesh(mesh.devices.reshape(SIZES), AXES)
    rows, columns = ("h", "x"), TENSOR
    placed = (P(rows, columns), P(columns, rows), P(rows, columns), P(columns), P(rows))
    return jax.shard_map(
        shards, mesh=fine, in_specs=placed, out_specs=P(columns, rows), check_vma=False
    )
```

```python
import math

import jax
import jax.numpy as jnp
import numpy as np
from jax import lax
from jax.experimental import pallas as pl
from jax.experimental.pallas import tpu as pltpu
from jax.sharding import Mesh, PartitionSpec as P

AXES = ("h", "x", "l", "yh", "yl", "c")
SIZES = (3, 4, 4, 4, 2, 2)
TENSOR = ("l", "yh", "yl", "c")
SLOTS = (0, 1, 3, 2)
WIDTH = 896
SPLIT = 384


def sine_coefficients():
    nodes = 0.25 * (1.0 + np.cos(np.pi * (np.arange(400) + 0.5) / 400)) ** 1.0
    squares = nodes**2
    target = np.sin(2.0 * np.pi * nodes) / (2.0 * np.pi)
    table = np.stack([nodes * squares**power for power in range(8)], axis=1)
    solved = np.linalg.lstsq(table, target, rcond=None)[0]
    return [float(entry) for entry in solved]


SINE = sine_coefficients()


def soft_round(values):
    rest = values - jnp.round(values)
    squares = rest * rest
    total = jnp.full_like(rest, SINE[-1])
    for entry in SINE[-2::-1]:
        total = total * squares + entry
    return values - rest * total


def walsh(order):
    indices = np.arange(order)
    shared = indices[:, None] & indices[None, :]
    parity = np.zeros((order, order), np.int64)
    for bit_level in range(order.bit_length() - 1):
        parity ^= shared >> bit_level & 1
    return (1 - 2 * parity).astype(np.float32)


def dot(left, right):
    return jnp.dot(left, right, preferred_element_type=jnp.float32)


def dot_transposed(left, right):
    return lax.dot_general(left, right, (((1,), (1,)), ((), ())), preferred_element_type=jnp.float32)


def ones_where(condition):
    return jnp.where(condition, 1.0, 0.0).astype(jnp.bfloat16)


def pack_kernel(hidden_ref, exponent_ref, index_ref, out_ref):
    scaling = jnp.exp2(exponent_ref[...].astype(jnp.float32)).astype(jnp.bfloat16)
    inverse = (1.0 / scaling.astype(jnp.float32)).astype(jnp.bfloat16)
    level = 7.5 - index_ref[...].astype(jnp.float32)
    lane = lax.broadcasted_iota(jnp.int32, (128, 64), 0)
    tail = dot(ones_where(lane == lax.broadcasted_iota(jnp.int32, (128, 64), 1)), hidden_ref[768:])
    lane = lax.broadcasted_iota(jnp.int32, (128, 13), 0)
    group = lax.broadcasted_iota(jnp.int32, (128, 13), 1)
    for kind, extra in enumerate((scaling, inverse)):
        tail += dot(ones_where(lane == group + (64 + 13 * kind)), extra)
    tail += jnp.sum(jnp.where(lane == group + 90, level, 0.0), axis=1, keepdims=True)
    tail = tail.astype(jnp.bfloat16)
    target = lax.broadcasted_iota(jnp.int32, (64, 128), 0)
    token = lax.broadcasted_iota(jnp.int32, (64, 128), 1)
    for which in range(2):
        chosen = ones_where(token == 2 * target + which)
        out_ref[:, which, :768] = dot_transposed(chosen, hidden_ref[:768]).astype(jnp.bfloat16)
        out_ref[:, which, 768:] = dot_transposed(chosen, tail).astype(jnp.bfloat16)


def pack(hidden, act_exponent, clip_index):
    return pl.pallas_call(
        pack_kernel,
        out_shape=jax.ShapeDtypeStruct((64, 2, WIDTH), jnp.bfloat16),
        in_specs=[pl.BlockSpec(memory_space=pltpu.VMEM)] * 3,
        out_specs=pl.BlockSpec(memory_space=pltpu.VMEM),
        compiler_params=pltpu.CompilerParams(vmem_limit_bytes=16 * 1024 * 1024),
        cost_estimate=pl.CostEstimate(flops=40_000_000, bytes_accessed=500_000, transcendentals=0),
    )(hidden.T, act_exponent.T, clip_index.reshape(1, 13))


def rotate_kernel(x_ref, rows_ref, lanes_ref, out_ref):
    lanes, rows = lanes_ref[...], rows_ref[...]
    row = lax.broadcasted_iota(jnp.int32, (128, 128), 0)
    upper = jnp.where(lax.broadcasted_iota(jnp.int32, (128, 128), 1) >= 64, 1, 0)
    place = row - upper
    for which in range(2):
        arrived = x_ref[:, which, :]
        mixed = dot(rows, arrived)
        extra = arrived[:, 768:896]
        for piece in range(7):
            width = 128 if piece < 6 else 64
            rest = mixed[:, piece * 128 : piece * 128 + 128]
            rotated = None
            for _ in range(3):
                part = rest.astype(jnp.bfloat16)
                rest = rest - part.astype(jnp.float32)
                term = dot(part, lanes)
                rotated = term if rotated is None else rotated + term
            scale, inverse, level = (
                dot(extra, ones_where(place == 64 + 13 * kind + 2 * piece)) for kind in range(3)
            )
            scaled = rotated * (1.0 / 64.0) * inverse
            clipped = jnp.maximum(jnp.minimum(scaled, level), -level)
            quantized = (soft_round(clipped) * scale).astype(jnp.bfloat16)
            out_ref[:, which, piece * 128 : piece * 128 + width] = quantized[:, :width]


def rotate_and_quantize(arrived):
    lanes = np.kron(np.eye(2, dtype=np.float32), walsh(64))
    return pl.pallas_call(
        rotate_kernel,
        out_shape=jax.ShapeDtypeStruct((64, 2, 832), jnp.bfloat16),
        in_specs=[pl.BlockSpec(memory_space=pltpu.VMEM)] * 3,
        out_specs=pl.BlockSpec(memory_space=pltpu.VMEM),
        compiler_params=pltpu.CompilerParams(vmem_limit_bytes=24 * 1024 * 1024),
        cost_estimate=pl.CostEstimate(flops=40_000_000_000, bytes_accessed=1_500_000, transcendentals=0),
    )(arrived, jnp.asarray(walsh(64), jnp.bfloat16), jnp.asarray(lanes, jnp.bfloat16))


def accumulate(acts, pieces):
    total, start = None, 0
    for piece in pieces:
        stop = start + piece.shape[0]
        term = jnp.dot(acts[:, start:stop], piece[...], preferred_element_type=jnp.float32)
        total = term if total is None else total + term
        start = stop
    return total


def product_kernel(counts, acts_ref, *refs):
    *pieces, other_ref, mine_ref = refs
    start = 0
    acts = acts_ref[...]
    for at, count in enumerate(counts):
        product = accumulate(acts, pieces[start : start + count])
        other_ref[at] = product[:192].astype(jnp.bfloat16)
        mine_ref[at] = product[192:]
        start += count


def products(acts, weights):
    flat = [piece for weight in weights for piece in weight]
    counts = tuple(len(weight) for weight in weights)
    return pl.pallas_call(
        lambda *refs: product_kernel(counts, *refs),
        out_shape=(
            jax.ShapeDtypeStruct((2, 192, 1024), jnp.bfloat16),
            jax.ShapeDtypeStruct((2, 192, 1024), jnp.float32),
        ),
        in_specs=[pl.BlockSpec(memory_space=pltpu.VMEM)] * (1 + len(flat)),
        out_specs=(pl.BlockSpec(memory_space=pltpu.VMEM),) * 2,
        compiler_params=pltpu.CompilerParams(vmem_limit_bytes=32 * 1024 * 1024),
        cost_estimate=pl.CostEstimate(flops=1_300_000_000, bytes_accessed=6_000_000, transcendentals=0),
    )(acts, *flat)


def arrange_kernel(source_ref, own_ref, next_1_ref, next_2_ref, out_ref):
    column = lax.broadcasted_iota(jnp.int32, (384, 64), 1)
    source = source_ref[...]
    total = None
    for at, rows_ref in enumerate((own_ref, next_1_ref, next_2_ref)):
        for which in range(2):
            term = dot(ones_where(source == 2 * column + (which + 128 * at)), rows_ref[:, which, :])
            total = term if total is None else total + term
    out_ref[...] = total.astype(jnp.bfloat16)


def arrange(source, own, next_1, next_2):
    return pl.pallas_call(
        arrange_kernel,
        out_shape=jax.ShapeDtypeStruct((384, 832), jnp.bfloat16),
        in_specs=[pl.BlockSpec(memory_space=pltpu.VMEM)] * 4,
        out_specs=pl.BlockSpec(memory_space=pltpu.VMEM),
        compiler_params=pltpu.CompilerParams(vmem_limit_bytes=16 * 1024 * 1024),
        cost_estimate=pl.CostEstimate(flops=20000000000, bytes_accessed=1_500_000, transcendentals=0),
    )(source, own, next_1, next_2)


def quantize_weight(weight_matrix, weight_exponent):
    scaling = jnp.exp2(weight_exponent.astype(jnp.float32)).astype(jnp.bfloat16).astype(jnp.float32)[None, :]
    clipped = jnp.clip(weight_matrix.astype(jnp.float32) / scaling, -7.5, 7.5)
    return (soft_round(clipped) * scaling).astype(jnp.bfloat16)


def ring(size, shift):
    return [(at, (at + shift) % size) for at in range(size)]


def final_pairs(which):
    pairs = []
    for x in range(4):
        for slot in range(4):
            for y in range(8):
                for c in range(2):
                    first = 3 * (2 * y + c)
                    if which == "main":
                        k = (first + 1) // 16
                    elif first // 16 != (first + 1) // 16:
                        k = first // 16
                    elif (first + 2) // 16 != (first + 1) // 16:
                        k = (first + 2) // 16
                    else:
                        continue
                    owner_l = (4 * ((k - x) % 3) + x) // 3
                    owner_x = (x + SLOTS[slot]) % 4
                    source = ((x * 4 + slot) * 8 + y) * 2 + c
                    pairs.append((source, ((owner_x * 4 + owner_l) * 8 + y) * 2 + c))
    return pairs


def row_order(h, x, y_low, c):
    at = lax.broadcasted_iota(jnp.int32, (384, 1), 0)
    core = jnp.where(at < 192, 1 - c, c)
    rest = at % 192
    parity = jnp.where(rest < 96, 1 - y_low, y_low)
    rest = rest % 96
    y = 2 * (rest // 24) + parity
    row = (2 * y + core) * 24 + rest % 24
    return (row - 128 * ((h + x) % 3) + 384) % 384


def shards(hidden, down_weight, act_exponent, clip_index, weight_exponent):
    h, x, y_low, c = (lax.axis_index(name) for name in ("h", "x", "yl", "c"))
    y_high = lax.axis_index("yh")

    def to_right(rows):
        return lax.ppermute(rows, "x", ring(4, 1))

    def to_left(rows):
        return lax.ppermute(rows, "x", ring(4, -1))

    packed = pack(hidden, act_exponent, clip_index)
    packed, down_weight = lax.optimization_barrier((packed, down_weight))
    weight_0 = quantize_weight(down_weight, weight_exponent)
    weight_1, weight_3 = to_left(weight_0), to_right(weight_0)
    arrived = lax.all_to_all(packed, TENSOR, split_axis=0, concat_axis=0, tiled=True)
    quantized = rotate_and_quantize(arrived)
    own = lax.all_to_all(quantized, TENSOR, split_axis=0, concat_axis=0, tiled=True)
    next_1 = lax.ppermute(own, "h", ring(3, -1))
    next_2 = lax.ppermute(own, "h", ring(3, 1))
    weight_2 = (to_right(weight_3[:SPLIT]), to_left(weight_1[SPLIT:]))
    acts = arrange(row_order(h, x, y_low, c), own, next_1, next_2)

    y_pairs_near = [(y, y ^ 1) for y in range(8)]
    y_pairs_far = [(y, (y - 1) % 8 if y % 2 == 0 else (y + 1) % 8) for y in range(8)]
    parts = []
    for weights, y_pairs in ((((weight_0,), (weight_1,)), y_pairs_near), (((weight_3,), weight_2), y_pairs_far)):
        other, own_rows = products(acts, weights)
        from_core = lax.ppermute(other, "c", [(0, 1), (1, 0)])
        mine = own_rows + from_core.astype(jnp.float32)
        from_y = lax.ppermute(mine[:, :96].astype(jnp.bfloat16), ("yh", "yl"), y_pairs)
        parts.append((mine[:, 96:] + from_y.astype(jnp.float32)).astype(jnp.bfloat16))
    sums = jnp.concatenate(parts, axis=0).reshape(16, 24, 1024)
    crossed = lax.all_to_all(sums, ("l", "yh"), split_axis=0, concat_axis=0, tiled=True)
    total = jnp.sum(crossed.astype(jnp.float32), axis=0).astype(jnp.bfloat16)

    y = 2 * y_high + y_low
    early = jnp.logical_and(y == 2, c == 1)
    late = jnp.logical_and(y == 5, c == 0)
    moved = lax.ppermute(total, ("x", "l", "yh", "yl", "c"), final_pairs("main"))
    fixed = lax.ppermute(
        jnp.where(early, total[:8], total[16:]), ("x", "l", "yh", "yl", "c"), final_pairs("fix")
    )
    return jnp.concatenate(
        [jnp.where(early, fixed, moved[:8]), moved[8:16], jnp.where(late, fixed, moved[16:])], axis=0
    )


def solution(mesh):
    fine = Mesh(mesh.devices.reshape(SIZES), AXES)
    rows, columns = ("h", "x"), TENSOR
    placed = (P(rows, columns), P(columns, rows), P(rows, columns), P(columns), P(rows))
    return jax.shard_map(
        shards, mesh=fine, in_specs=placed, out_specs=P(columns, rows), check_vma=False
    )
```

```python
import math

import jax
import jax.numpy as jnp
import numpy as np
from jax import lax
from jax.experimental import pallas as pl
from jax.experimental.pallas import tpu as pltpu
from jax.sharding import Mesh, PartitionSpec as P

AXES = ("h", "x", "l", "yh", "yl", "c")
SIZES = (3, 4, 4, 4, 2, 2)
TENSOR = ("l", "yh", "yl", "c")
SLOTS = (0, 1, 3, 2)
WIDTH = 896
SPLIT = 384


def sine_coefficients():
    nodes = 0.25 * (1.0 + np.cos(np.pi * (np.arange(400) + 0.5) / 400)) ** 1.0
    squares = nodes**2
    target = np.sin(2.0 * np.pi * nodes) / (2.0 * np.pi)
    table = np.stack([nodes * squares**power for power in range(8)], axis=1)
    solved = np.linalg.lstsq(table, target, rcond=None)[0]
    return [float(entry) for entry in solved]


SINE = sine_coefficients()


def soft_round(values):
    rest = values - jnp.round(values)
    squares = rest * rest
    total = jnp.full_like(rest, SINE[-1])
    for entry in SINE[-2::-1]:
        total = total * squares + entry
    return values - rest * total


def walsh(order):
    indices = np.arange(order)
    shared = indices[:, None] & indices[None, :]
    parity = np.zeros((order, order), np.int64)
    for bit_level in range(order.bit_length() - 1):
        parity ^= shared >> bit_level & 1
    return (1 - 2 * parity).astype(np.float32)


def dot(left, right):
    return jnp.dot(left, right, preferred_element_type=jnp.float32)


def dot_transposed(left, right):
    return lax.dot_general(left, right, (((1,), (1,)), ((), ())), preferred_element_type=jnp.float32)


def ones_where(condition):
    return jnp.where(condition, 1.0, 0.0).astype(jnp.bfloat16)


def pack_kernel(hidden_ref, exponent_ref, index_ref, out_ref):
    scaling = jnp.exp2(exponent_ref[...].astype(jnp.float32)).astype(jnp.bfloat16)
    inverse = (1.0 / scaling.astype(jnp.float32)).astype(jnp.bfloat16)
    level = 7.5 - index_ref[...].astype(jnp.float32)
    lane = lax.broadcasted_iota(jnp.int32, (128, 64), 0)
    tail = dot(ones_where(lane == lax.broadcasted_iota(jnp.int32, (128, 64), 1)), hidden_ref[768:])
    lane = lax.broadcasted_iota(jnp.int32, (128, 13), 0)
    group = lax.broadcasted_iota(jnp.int32, (128, 13), 1)
    for kind, extra in enumerate((scaling, inverse)):
        tail += dot(ones_where(lane == group + (64 + 13 * kind)), extra)
    tail += jnp.sum(jnp.where(lane == group + 90, level, 0.0), axis=1, keepdims=True)
    tail = tail.astype(jnp.bfloat16)
    target = lax.broadcasted_iota(jnp.int32, (64, 128), 0)
    token = lax.broadcasted_iota(jnp.int32, (64, 128), 1)
    for which in range(2):
        chosen = ones_where(token == 2 * target + which)
        out_ref[:, which, :768] = dot_transposed(chosen, hidden_ref[:768]).astype(jnp.bfloat16)
        out_ref[:, which, 768:] = dot_transposed(chosen, tail).astype(jnp.bfloat16)


def pack(hidden, act_exponent, clip_index):
    return pl.pallas_call(
        pack_kernel,
        out_shape=jax.ShapeDtypeStruct((64, 2, WIDTH), jnp.bfloat16),
        in_specs=[pl.BlockSpec(memory_space=pltpu.VMEM)] * 3,
        out_specs=pl.BlockSpec(memory_space=pltpu.VMEM),
        compiler_params=pltpu.CompilerParams(vmem_limit_bytes=16 * 1024 * 1024),
        cost_estimate=pl.CostEstimate(flops=40_000_000, bytes_accessed=500_000, transcendentals=0),
    )(hidden.T, act_exponent.T, clip_index.reshape(1, 13))


def rotate_kernel(x_ref, rows_ref, lanes_ref, out_ref):
    lanes = lanes_ref[...]
    row = lax.broadcasted_iota(jnp.int32, (128, 128), 0)
    upper = jnp.where(lax.broadcasted_iota(jnp.int32, (128, 128), 1) >= 64, 1, 0)
    place = row - upper
    arrived = x_ref[...].reshape(128, WIDTH)
    mixed = dot(rows_ref[...], arrived)
    extra = arrived[:, 768:896]
    for piece in range(7):
        width = 128 if piece < 6 else 64
        rest = mixed[:, piece * 128 : piece * 128 + 128]
        rotated = None
        for _ in range(3):
            part = rest.astype(jnp.bfloat16)
            rest = rest - part.astype(jnp.float32)
            term = dot(part, lanes)
            rotated = term if rotated is None else rotated + term
        scale, inverse, level = (
            dot(extra, ones_where(place == 64 + 13 * kind + 2 * piece)) for kind in range(3)
        )
        scaled = rotated * (1.0 / 64.0) * inverse
        clipped = jnp.maximum(jnp.minimum(scaled, level), -level)
        quantized = (soft_round(clipped) * scale).astype(jnp.bfloat16)
        out_ref[:, :, piece * 128 : piece * 128 + width] = quantized[:, :width].reshape(64, 2, width)


def rotate_and_quantize(arrived):
    lanes = np.kron(np.eye(2, dtype=np.float32), walsh(64))
    return pl.pallas_call(
        rotate_kernel,
        out_shape=jax.ShapeDtypeStruct((64, 2, 832), jnp.bfloat16),
        in_specs=[pl.BlockSpec(memory_space=pltpu.VMEM)] * 3,
        out_specs=pl.BlockSpec(memory_space=pltpu.VMEM),
        compiler_params=pltpu.CompilerParams(vmem_limit_bytes=24 * 1024 * 1024),
        cost_estimate=pl.CostEstimate(flops=2_000_000_000, bytes_accessed=1_500_000, transcendentals=0),
    )(arrived, jnp.asarray(np.kron(walsh(64), np.eye(2)), jnp.bfloat16), jnp.asarray(lanes, jnp.bfloat16))


def accumulate(acts, pieces):
    total, start = None, 0
    for piece in pieces:
        stop = start + piece.shape[0]
        term = jnp.dot(acts[:, start:stop], piece[...], preferred_element_type=jnp.float32)
        total = term if total is None else total + term
        start = stop
    return total


def product_kernel(counts, acts_ref, *refs):
    *pieces, other_ref, mine_ref = refs
    start = 0
    acts = acts_ref[...]
    for at, count in enumerate(counts):
        product = accumulate(acts, pieces[start : start + count])
        other_ref[at] = product[:192].astype(jnp.bfloat16)
        mine_ref[at] = product[192:]
        start += count


def products(acts, weights):
    flat = [piece for weight in weights for piece in weight]
    counts = tuple(len(weight) for weight in weights)
    return pl.pallas_call(
        lambda *refs: product_kernel(counts, *refs),
        out_shape=(
            jax.ShapeDtypeStruct((2, 192, 1024), jnp.bfloat16),
            jax.ShapeDtypeStruct((2, 192, 1024), jnp.float32),
        ),
        in_specs=[pl.BlockSpec(memory_space=pltpu.VMEM)] * (1 + len(flat)),
        out_specs=(pl.BlockSpec(memory_space=pltpu.VMEM),) * 2,
        compiler_params=pltpu.CompilerParams(vmem_limit_bytes=32 * 1024 * 1024),
        cost_estimate=pl.CostEstimate(flops=1_300_000_000, bytes_accessed=6_000_000, transcendentals=0),
    )(acts, *flat)


def arrange_kernel(source_ref, own_ref, next_1_ref, next_2_ref, out_ref):
    column = lax.broadcasted_iota(jnp.int32, (384, 128), 1)
    source = source_ref[...]
    total = None
    for at, rows_ref in enumerate((own_ref, next_1_ref, next_2_ref)):
        term = dot(ones_where(source == column + 128 * at), rows_ref[...].reshape(128, 832))
        total = term if total is None else total + term
    out_ref[...] = total.astype(jnp.bfloat16)


def arrange(source, own, next_1, next_2):
    return pl.pallas_call(
        arrange_kernel,
        out_shape=jax.ShapeDtypeStruct((384, 832), jnp.bfloat16),
        in_specs=[pl.BlockSpec(memory_space=pltpu.VMEM)] * 4,
        out_specs=pl.BlockSpec(memory_space=pltpu.VMEM),
        compiler_params=pltpu.CompilerParams(vmem_limit_bytes=16 * 1024 * 1024),
        cost_estimate=pl.CostEstimate(flops=20000000000, bytes_accessed=1_500_000, transcendentals=0),
    )(source, own, next_1, next_2)


def quantize_weight(weight_matrix, weight_exponent):
    scaling = jnp.exp2(weight_exponent.astype(jnp.float32)).astype(jnp.bfloat16).astype(jnp.float32)[None, :]
    clipped = jnp.clip(weight_matrix.astype(jnp.float32) / scaling, -7.5, 7.5)
    return (soft_round(clipped) * scaling).astype(jnp.bfloat16)


def ring(size, shift):
    return [(at, (at + shift) % size) for at in range(size)]


def final_pairs(which):
    pairs = []
    for x in range(4):
        for slot in range(4):
            for y in range(8):
                for c in range(2):
                    first = 3 * (2 * y + c)
                    if which == "main":
                        k = (first + 1) // 16
                    elif first // 16 != (first + 1) // 16:
                        k = first // 16
                    elif (first + 2) // 16 != (first + 1) // 16:
                        k = (first + 2) // 16
                    else:
                        continue
                    owner_l = (4 * ((k - x) % 3) + x) // 3
                    owner_x = (x + SLOTS[slot]) % 4
                    source = ((x * 4 + slot) * 8 + y) * 2 + c
                    pairs.append((source, ((owner_x * 4 + owner_l) * 8 + y) * 2 + c))
    return pairs


def row_order(h, x, y_low, c):
    at = lax.broadcasted_iota(jnp.int32, (384, 1), 0)
    core = jnp.where(at < 192, 1 - c, c)
    rest = at % 192
    parity = jnp.where(rest < 96, 1 - y_low, y_low)
    rest = rest % 96
    y = 2 * (rest // 24) + parity
    row = (2 * y + core) * 24 + rest % 24
    return (row - 128 * ((h + x) % 3) + 384) % 384


def shards(hidden, down_weight, act_exponent, clip_index, weight_exponent):
    h, x, y_low, c = (lax.axis_index(name) for name in ("h", "x", "yl", "c"))
    y_high = lax.axis_index("yh")

    def to_right(rows):
        return lax.ppermute(rows, "x", ring(4, 1))

    def to_left(rows):
        return lax.ppermute(rows, "x", ring(4, -1))

    packed = pack(hidden, act_exponent, clip_index)
    packed, down_weight = lax.optimization_barrier((packed, down_weight))
    weight_0 = quantize_weight(down_weight, weight_exponent)
    weight_1, weight_3 = to_left(weight_0), to_right(weight_0)
    arrived = lax.all_to_all(packed, TENSOR, split_axis=0, concat_axis=0, tiled=True)
    quantized = rotate_and_quantize(arrived)
    own = lax.all_to_all(quantized, TENSOR, split_axis=0, concat_axis=0, tiled=True)
    next_1 = lax.ppermute(own, "h", ring(3, -1))
    next_2 = lax.ppermute(own, "h", ring(3, 1))
    weight_2 = (to_right(weight_3[:SPLIT]), to_left(weight_1[SPLIT:]))
    acts = arrange(row_order(h, x, y_low, c), own, next_1, next_2)

    y_pairs_near = [(y, y ^ 1) for y in range(8)]
    y_pairs_far = [(y, (y - 1) % 8 if y % 2 == 0 else (y + 1) % 8) for y in range(8)]
    parts = []
    for weights, y_pairs in ((((weight_0,), (weight_1,)), y_pairs_near), (((weight_3,), weight_2), y_pairs_far)):
        other, own_rows = products(acts, weights)
        from_core = lax.ppermute(other, "c", [(0, 1), (1, 0)])
        mine = own_rows + from_core.astype(jnp.float32)
        from_y = lax.ppermute(mine[:, :96].astype(jnp.bfloat16), ("yh", "yl"), y_pairs)
        parts.append((mine[:, 96:] + from_y.astype(jnp.float32)).astype(jnp.bfloat16))
    sums = jnp.concatenate(parts, axis=0).reshape(16, 24, 1024)
    crossed = lax.all_to_all(sums, ("l", "yh"), split_axis=0, concat_axis=0, tiled=True)
    total = jnp.sum(crossed.astype(jnp.float32), axis=0).astype(jnp.bfloat16)

    y = 2 * y_high + y_low
    early = jnp.logical_and(y == 2, c == 1)
    late = jnp.logical_and(y == 5, c == 0)
    moved = lax.ppermute(total, ("x", "l", "yh", "yl", "c"), final_pairs("main"))
    fixed = lax.ppermute(
        jnp.where(early, total[:8], total[16:]), ("x", "l", "yh", "yl", "c"), final_pairs("fix")
    )
    return jnp.concatenate(
        [jnp.where(early, fixed, moved[:8]), moved[8:16], jnp.where(late, fixed, moved[16:])], axis=0
    )


def solution(mesh):
    fine = Mesh(mesh.devices.reshape(SIZES), AXES)
    rows, columns = ("h", "x"), TENSOR
    placed = (P(rows, columns), P(columns, rows), P(rows, columns), P(columns), P(rows))
    return jax.shard_map(
        shards, mesh=fine, in_specs=placed, out_specs=P(columns, rows), check_vma=False
    )
```

```python
import math

import jax
import jax.numpy as jnp
import numpy as np
from jax import lax
from jax.experimental import pallas as pl
from jax.experimental.pallas import tpu as pltpu
from jax.sharding import Mesh, PartitionSpec as P

AXES = ("h", "x", "l", "yh", "yl", "c")
SIZES = (3, 4, 4, 4, 2, 2)
TENSOR = ("l", "yh", "yl", "c")
SLOTS = (0, 1, 3, 2)
WIDTH = 896
SPLIT = 384


def sine_coefficients():
    nodes = 0.25 * (1.0 + np.cos(np.pi * (np.arange(400) + 0.5) / 400)) ** 1.0
    squares = nodes**2
    target = np.sin(2.0 * np.pi * nodes) / (2.0 * np.pi)
    table = np.stack([nodes * squares**power for power in range(8)], axis=1)
    solved = np.linalg.lstsq(table, target, rcond=None)[0]
    return [float(entry) for entry in solved]


SINE = sine_coefficients()


def soft_round(values):
    rest = values - jnp.round(values)
    squares = rest * rest
    total = jnp.full_like(rest, SINE[-1])
    for entry in SINE[-2::-1]:
        total = total * squares + entry
    return values - rest * total


def walsh(order):
    indices = np.arange(order)
    shared = indices[:, None] & indices[None, :]
    parity = np.zeros((order, order), np.int64)
    for bit_level in range(order.bit_length() - 1):
        parity ^= shared >> bit_level & 1
    return (1 - 2 * parity).astype(np.float32)


def dot(left, right):
    return jnp.dot(left, right, preferred_element_type=jnp.float32)


def dot_transposed(left, right):
    return lax.dot_general(left, right, (((1,), (1,)), ((), ())), preferred_element_type=jnp.float32)


def ones_where(condition):
    return jnp.where(condition, 1.0, 0.0).astype(jnp.bfloat16)


def pack_kernel(hidden_ref, exponent_ref, index_ref, out_ref):
    scaling = jnp.exp2(exponent_ref[...].astype(jnp.float32)).astype(jnp.bfloat16)
    inverse = (1.0 / scaling.astype(jnp.float32)).astype(jnp.bfloat16)
    level = 7.5 - index_ref[...].astype(jnp.float32)
    lane = lax.broadcasted_iota(jnp.int32, (128, 64), 0)
    tail = dot(ones_where(lane == lax.broadcasted_iota(jnp.int32, (128, 64), 1)), hidden_ref[768:])
    lane = lax.broadcasted_iota(jnp.int32, (128, 13), 0)
    group = lax.broadcasted_iota(jnp.int32, (128, 13), 1)
    for kind, extra in enumerate((scaling, inverse)):
        tail += dot(ones_where(lane == group + (64 + 13 * kind)), extra)
    tail += jnp.sum(jnp.where(lane == group + 90, level, 0.0), axis=1, keepdims=True)
    tail = tail.astype(jnp.bfloat16)
    target = lax.broadcasted_iota(jnp.int32, (64, 128), 0)
    token = lax.broadcasted_iota(jnp.int32, (64, 128), 1)
    for which in range(2):
        chosen = ones_where(token == 2 * target + which)
        out_ref[:, which, :768] = dot_transposed(chosen, hidden_ref[:768]).astype(jnp.bfloat16)
        out_ref[:, which, 768:] = dot_transposed(chosen, tail).astype(jnp.bfloat16)


def pack(hidden, act_exponent, clip_index):
    return pl.pallas_call(
        pack_kernel,
        out_shape=jax.ShapeDtypeStruct((64, 2, WIDTH), jnp.bfloat16),
        in_specs=[pl.BlockSpec(memory_space=pltpu.VMEM)] * 3,
        out_specs=pl.BlockSpec(memory_space=pltpu.VMEM),
        compiler_params=pltpu.CompilerParams(vmem_limit_bytes=16 * 1024 * 1024),
        cost_estimate=pl.CostEstimate(flops=40_000_000, bytes_accessed=500_000, transcendentals=0),
    )(hidden.T, act_exponent.T, clip_index.reshape(1, 13))


def rotate_kernel(x_ref, rows_ref, lanes_ref, out_ref):
    lanes = lanes_ref[...]
    row = lax.broadcasted_iota(jnp.int32, (128, 128), 0)
    upper = jnp.where(lax.broadcasted_iota(jnp.int32, (128, 128), 1) >= 64, 1, 0)
    place = row - upper
    arrived = x_ref[...].reshape(128, WIDTH)
    mixed = dot(rows_ref[...], arrived)
    extra = arrived[:, 768:896]
    for piece in range(7):
        width = 128 if piece < 6 else 64
        rest = mixed[:, piece * 128 : piece * 128 + 128]
        rotated = None
        for _ in range(3):
            part = rest.astype(jnp.bfloat16)
            rest = rest - part.astype(jnp.float32)
            term = dot(part, lanes)
            rotated = term if rotated is None else rotated + term
        scale, inverse, level = (
            dot(extra, ones_where(place == 64 + 13 * kind + 2 * piece)) for kind in range(3)
        )
        scaled = rotated * (1.0 / 64.0) * inverse
        clipped = jnp.maximum(jnp.minimum(scaled, level), -level)
        quantized = (soft_round(clipped) * scale).astype(jnp.bfloat16)
        out_ref[:, :, piece * 128 : piece * 128 + width] = quantized[:, :width].reshape(64, 2, width)


def rotate_and_quantize(arrived):
    lanes = np.kron(np.eye(2, dtype=np.float32), walsh(64))
    return pl.pallas_call(
        rotate_kernel,
        out_shape=jax.ShapeDtypeStruct((64, 2, 832), jnp.bfloat16),
        in_specs=[pl.BlockSpec(memory_space=pltpu.VMEM)] * 3,
        out_specs=pl.BlockSpec(memory_space=pltpu.VMEM),
        compiler_params=pltpu.CompilerParams(vmem_limit_bytes=24 * 1024 * 1024),
        cost_estimate=pl.CostEstimate(flops=2_000_000_000, bytes_accessed=1_500_000, transcendentals=0),
    )(arrived, jnp.asarray(np.kron(walsh(64), np.eye(2)), jnp.bfloat16), jnp.asarray(lanes, jnp.bfloat16))


def accumulate(acts, pieces):
    total, start = None, 0
    for piece in pieces:
        stop = start + piece.shape[0]
        term = jnp.dot(acts[:, start:stop], piece[...], preferred_element_type=jnp.float32)
        total = term if total is None else total + term
        start = stop
    return total


def first_kernel(acts_ref, near_0_ref, near_1_ref, far_ref, other_ref, mine_ref, far_other_ref, far_mine_ref):
    acts = acts_ref[...]
    for at, weight_ref in enumerate((near_0_ref, near_1_ref, far_ref)):
        product = dot(acts, weight_ref[...])
        if at < 2:
            other_ref[at] = product[:192].astype(jnp.bfloat16)
            mine_ref[at] = product[192:]
        else:
            far_other_ref[0] = product[:192].astype(jnp.bfloat16)
            far_mine_ref[0] = product[192:]


def last_kernel(acts_ref, top_ref, low_ref, far_other_in, far_mine_in, far_other_ref, far_mine_ref):
    product = accumulate(acts_ref[...], (top_ref, low_ref))
    far_other_ref[0] = far_other_in[0]
    far_mine_ref[0] = far_mine_in[0]
    far_other_ref[1] = product[:192].astype(jnp.bfloat16)
    far_mine_ref[1] = product[192:]


def products(kernel, shapes, operands, flops):
    return pl.pallas_call(
        kernel,
        out_shape=tuple(
            jax.ShapeDtypeStruct((count, 192, 1024), kind) for count in shapes for kind in (jnp.bfloat16, jnp.float32)
        ),
        in_specs=[pl.BlockSpec(memory_space=pltpu.VMEM)] * len(operands),
        out_specs=(pl.BlockSpec(memory_space=pltpu.VMEM),) * (2 * len(shapes)),
        compiler_params=pltpu.CompilerParams(vmem_limit_bytes=32 * 1024 * 1024),
        cost_estimate=pl.CostEstimate(flops=flops, bytes_accessed=6_000_000, transcendentals=0),
    )(*operands)


def arrange_kernel(source_ref, own_ref, next_1_ref, next_2_ref, out_ref):
    column = lax.broadcasted_iota(jnp.int32, (384, 128), 1)
    source = source_ref[...]
    total = None
    for at, rows_ref in enumerate((own_ref, next_1_ref, next_2_ref)):
        term = dot(ones_where(source == column + 128 * at), rows_ref[...].reshape(128, 832))
        total = term if total is None else total + term
    out_ref[...] = total.astype(jnp.bfloat16)


def arrange(source, own, next_1, next_2):
    return pl.pallas_call(
        arrange_kernel,
        out_shape=jax.ShapeDtypeStruct((384, 832), jnp.bfloat16),
        in_specs=[pl.BlockSpec(memory_space=pltpu.VMEM)] * 4,
        out_specs=pl.BlockSpec(memory_space=pltpu.VMEM),
        compiler_params=pltpu.CompilerParams(vmem_limit_bytes=16 * 1024 * 1024),
        cost_estimate=pl.CostEstimate(flops=20000000000, bytes_accessed=1_500_000, transcendentals=0),
    )(source, own, next_1, next_2)


def quantize_weight(weight_matrix, weight_exponent):
    coarse = (weight_exponent == -8)[None, :]
    scaling = jnp.where(coarse, 2.0**-8, 2.0**-9)
    clipped = jnp.clip(weight_matrix.astype(jnp.float32) * jnp.where(coarse, 2.0**8, 2.0**9), -7.5, 7.5)
    return (soft_round(clipped) * scaling).astype(jnp.bfloat16)


def ring(size, shift):
    return [(at, (at + shift) % size) for at in range(size)]


def final_pairs(which):
    pairs = []
    for x in range(4):
        for slot in range(4):
            for y in range(8):
                for c in range(2):
                    first = 3 * (2 * y + c)
                    if which == "main":
                        k = (first + 1) // 16
                    elif first // 16 != (first + 1) // 16:
                        k = first // 16
                    elif (first + 2) // 16 != (first + 1) // 16:
                        k = (first + 2) // 16
                    else:
                        continue
                    owner_l = (4 * ((k - x) % 3) + x) // 3
                    owner_x = (x + SLOTS[slot]) % 4
                    source = ((x * 4 + slot) * 8 + y) * 2 + c
                    pairs.append((source, ((owner_x * 4 + owner_l) * 8 + y) * 2 + c))
    return pairs


def row_order(h, x, y_low, c):
    at = lax.broadcasted_iota(jnp.int32, (384, 1), 0)
    core = jnp.where(at < 192, 1 - c, c)
    rest = at % 192
    parity = jnp.where(rest < 96, 1 - y_low, y_low)
    rest = rest % 96
    y = 2 * (rest // 24) + parity
    row = (2 * y + core) * 24 + rest % 24
    return (row - 128 * ((h + x) % 3) + 384) % 384


def shards(hidden, down_weight, act_exponent, clip_index, weight_exponent):
    h, x, y_low, c = (lax.axis_index(name) for name in ("h", "x", "yl", "c"))
    y_high = lax.axis_index("yh")

    def to_right(rows):
        return lax.ppermute(rows, "x", ring(4, 1))

    def to_left(rows):
        return lax.ppermute(rows, "x", ring(4, -1))

    packed = pack(hidden, act_exponent, clip_index)
    packed, down_weight = lax.optimization_barrier((packed, down_weight))
    weight_0 = quantize_weight(down_weight, weight_exponent)
    weight_1, weight_3 = to_left(weight_0), to_right(weight_0)
    arrived = lax.all_to_all(packed, TENSOR, split_axis=0, concat_axis=0, tiled=True)
    quantized = rotate_and_quantize(arrived)
    own = lax.all_to_all(quantized, TENSOR, split_axis=0, concat_axis=0, tiled=True)
    next_1 = lax.ppermute(own, "h", ring(3, -1))
    next_2 = lax.ppermute(own, "h", ring(3, 1))
    weight_2 = (to_right(weight_3[:SPLIT]), to_left(weight_1[SPLIT:]))
    acts = arrange(row_order(h, x, y_low, c), own, next_1, next_2)

    y_pairs_near = [(y, y ^ 1) for y in range(8)]
    y_pairs_far = [(y, (y - 1) % 8 if y % 2 == 0 else (y + 1) % 8) for y in range(8)]
    def over_core(other, own_rows):
        return own_rows + lax.ppermute(other, "c", [(0, 1), (1, 0)]).astype(jnp.float32)

    def over_y(mine, y_pairs):
        from_y = lax.ppermute(mine[:, :96].astype(jnp.bfloat16), ("yh", "yl"), y_pairs)
        return (mine[:, 96:] + from_y.astype(jnp.float32)).astype(jnp.bfloat16)

    other, own_rows, far_other, far_rows = products(
        first_kernel, (2, 1), (acts, weight_0, weight_1, weight_3), 1_300_000_000
    )
    near = over_core(other, own_rows)
    far_other, far_rows = products(last_kernel, (2,), (acts, *weight_2, far_other, far_rows), 1_300_000_000)
    far = over_core(far_other, far_rows)
    parts = [over_y(near, y_pairs_near), over_y(far, y_pairs_far)]
    sums = jnp.concatenate(parts, axis=0).reshape(16, 24, 1024)
    crossed = lax.all_to_all(sums, ("l", "yh"), split_axis=0, concat_axis=0, tiled=True)
    total = jnp.sum(crossed.astype(jnp.float32), axis=0).astype(jnp.bfloat16)

    y = 2 * y_high + y_low
    early = jnp.logical_and(y == 2, c == 1)
    late = jnp.logical_and(y == 5, c == 0)
    moved = lax.ppermute(total, ("x", "l", "yh", "yl", "c"), final_pairs("main"))
    fixed = lax.ppermute(
        jnp.where(early, total[:8], total[16:]), ("x", "l", "yh", "yl", "c"), final_pairs("fix")
    )
    return jnp.concatenate(
        [jnp.where(early, fixed, moved[:8]), moved[8:16], jnp.where(late, fixed, moved[16:])], axis=0
    )


def solution(mesh):
    fine = Mesh(mesh.devices.reshape(SIZES), AXES)
    rows, columns = ("h", "x"), TENSOR
    placed = (P(rows, columns), P(columns, rows), P(rows, columns), P(columns), P(rows))
    return jax.shard_map(
        shards, mesh=fine, in_specs=placed, out_specs=P(columns, rows), check_vma=False
    )
```

```python
import math

import jax
import jax.numpy as jnp
import numpy as np
from jax import lax
from jax.experimental import pallas as pl
from jax.experimental.pallas import tpu as pltpu
from jax.sharding import Mesh, PartitionSpec as P

AXES = ("h", "x", "l", "yh", "yl", "c")
SIZES = (3, 4, 4, 4, 2, 2)
TENSOR = ("l", "yh", "yl", "c")
SLOTS = (0, 1, 3, 2)
WIDTH = 896
SPLIT = 384


def sine_coefficients():
    nodes = 0.25 * (1.0 + np.cos(np.pi * (np.arange(400) + 0.5) / 400)) ** 1.0
    squares = nodes**2
    target = np.sin(2.0 * np.pi * nodes) / (2.0 * np.pi)
    table = np.stack([nodes * squares**power for power in range(8)], axis=1)
    solved = np.linalg.lstsq(table, target, rcond=None)[0]
    return [float(entry) for entry in solved]


SINE = sine_coefficients()


def soft_round(values):
    rest = values - jnp.round(values)
    squares = rest * rest
    total = jnp.full_like(rest, SINE[-1])
    for entry in SINE[-2::-1]:
        total = total * squares + entry
    return values - rest * total


def walsh(order):
    indices = np.arange(order)
    shared = indices[:, None] & indices[None, :]
    parity = np.zeros((order, order), np.int64)
    for bit_level in range(order.bit_length() - 1):
        parity ^= shared >> bit_level & 1
    return (1 - 2 * parity).astype(np.float32)


def dot(left, right):
    return jnp.dot(left, right, preferred_element_type=jnp.float32)


def dot_transposed(left, right):
    return lax.dot_general(left, right, (((1,), (1,)), ((), ())), preferred_element_type=jnp.float32)


def ones_where(condition):
    return jnp.where(condition, 1.0, 0.0).astype(jnp.bfloat16)


def pack_kernel(hidden_ref, exponent_ref, index_ref, out_ref):
    scaling = jnp.exp2(exponent_ref[...].astype(jnp.float32)).astype(jnp.bfloat16)
    inverse = (1.0 / scaling.astype(jnp.float32)).astype(jnp.bfloat16)
    level = 7.5 - index_ref[...].astype(jnp.float32)
    lane = lax.broadcasted_iota(jnp.int32, (128, 64), 0)
    tail = dot(ones_where(lane == lax.broadcasted_iota(jnp.int32, (128, 64), 1)), hidden_ref[768:])
    lane = lax.broadcasted_iota(jnp.int32, (128, 13), 0)
    group = lax.broadcasted_iota(jnp.int32, (128, 13), 1)
    for kind, extra in enumerate((scaling, inverse)):
        tail += dot(ones_where(lane == group + (64 + 13 * kind)), extra)
    tail += jnp.sum(jnp.where(lane == group + 90, level, 0.0), axis=1, keepdims=True)
    tail = tail.astype(jnp.bfloat16)
    target = lax.broadcasted_iota(jnp.int32, (64, 128), 0)
    token = lax.broadcasted_iota(jnp.int32, (64, 128), 1)
    for which in range(2):
        chosen = ones_where(token == 2 * target + which)
        out_ref[:, which, :768] = dot_transposed(chosen, hidden_ref[:768]).astype(jnp.bfloat16)
        out_ref[:, which, 768:] = dot_transposed(chosen, tail).astype(jnp.bfloat16)


def pack(hidden, act_exponent, clip_index):
    return pl.pallas_call(
        pack_kernel,
        out_shape=jax.ShapeDtypeStruct((64, 2, WIDTH), jnp.bfloat16),
        in_specs=[pl.BlockSpec(memory_space=pltpu.VMEM)] * 3,
        out_specs=pl.BlockSpec(memory_space=pltpu.VMEM),
        compiler_params=pltpu.CompilerParams(vmem_limit_bytes=16 * 1024 * 1024),
        cost_estimate=pl.CostEstimate(flops=40_000_000, bytes_accessed=500_000, transcendentals=0),
    )(hidden.T, act_exponent.T, clip_index.reshape(1, 13))


def rotate_kernel(x_ref, rows_ref, lanes_ref, out_ref):
    lanes = lanes_ref[...]
    row = lax.broadcasted_iota(jnp.int32, (128, 128), 0)
    upper = jnp.where(lax.broadcasted_iota(jnp.int32, (128, 128), 1) >= 64, 1, 0)
    place = row - upper
    arrived = x_ref[...].reshape(128, WIDTH)
    mixed = dot(rows_ref[...], arrived)
    extra = arrived[:, 768:896]
    for piece in range(7):
        width = 128 if piece < 6 else 64
        rest = mixed[:, piece * 128 : piece * 128 + 128]
        rotated = None
        for _ in range(3):
            part = rest.astype(jnp.bfloat16)
            rest = rest - part.astype(jnp.float32)
            term = dot(part, lanes)
            rotated = term if rotated is None else rotated + term
        scale, inverse, level = (
            dot(extra, ones_where(place == 64 + 13 * kind + 2 * piece)) for kind in range(3)
        )
        scaled = rotated * (1.0 / 64.0) * inverse
        clipped = jnp.maximum(jnp.minimum(scaled, level), -level)
        quantized = (soft_round(clipped) * scale).astype(jnp.bfloat16)
        out_ref[:, :, piece * 128 : piece * 128 + width] = quantized[:, :width].reshape(64, 2, width)


def rotate_and_quantize(arrived):
    lanes = np.kron(np.eye(2, dtype=np.float32), walsh(64))
    return pl.pallas_call(
        rotate_kernel,
        out_shape=jax.ShapeDtypeStruct((64, 2, 832), jnp.bfloat16),
        in_specs=[pl.BlockSpec(memory_space=pltpu.VMEM)] * 3,
        out_specs=pl.BlockSpec(memory_space=pltpu.VMEM),
        compiler_params=pltpu.CompilerParams(vmem_limit_bytes=24 * 1024 * 1024),
        cost_estimate=pl.CostEstimate(flops=20_000_000_000, bytes_accessed=1_500_000, transcendentals=0),
    )(arrived, jnp.asarray(np.kron(walsh(64), np.eye(2)), jnp.bfloat16), jnp.asarray(lanes, jnp.bfloat16))


def accumulate(acts, pieces):
    total, start = None, 0
    for piece in pieces:
        stop = start + piece.shape[0]
        term = jnp.dot(acts[:, start:stop], piece[...], preferred_element_type=jnp.float32)
        total = term if total is None else total + term
        start = stop
    return total


def take_rows(weight, start, stop):
    def kernel(weight_ref, out_ref):
        out_ref[...] = weight_ref[start:stop]

    return pl.pallas_call(
        kernel,
        out_shape=jax.ShapeDtypeStruct((stop - start, 1024), jnp.bfloat16),
        in_specs=[pl.BlockSpec(memory_space=pltpu.VMEM)],
        out_specs=pl.BlockSpec(memory_space=pltpu.VMEM),
        compiler_params=pltpu.CompilerParams(vmem_limit_bytes=8 * 1024 * 1024),
        cost_estimate=pl.CostEstimate(flops=20_000_000_000, bytes_accessed=1_700_000, transcendentals=0),
    )(weight)


def first_kernel(acts_ref, near_0_ref, near_1_ref, far_ref, other_ref, mine_ref, far_other_ref, far_mine_ref):
    acts = acts_ref[...]
    for at, weight_ref in enumerate((near_0_ref, near_1_ref, far_ref)):
        product = dot(acts, weight_ref[...])
        if at < 2:
            other_ref[at] = product[:192].astype(jnp.bfloat16)
            mine_ref[at] = product[192:]
        else:
            far_other_ref[0] = product[:192].astype(jnp.bfloat16)
            far_mine_ref[0] = product[192:]


def last_kernel(acts_ref, top_ref, low_ref, far_other_in, far_mine_in, far_other_ref, far_mine_ref):
    product = accumulate(acts_ref[...], (top_ref, low_ref))
    far_other_ref[0] = far_other_in[0]
    far_mine_ref[0] = far_mine_in[0]
    far_other_ref[1] = product[:192].astype(jnp.bfloat16)
    far_mine_ref[1] = product[192:]


def products(kernel, shapes, operands, flops):
    return pl.pallas_call(
        kernel,
        out_shape=tuple(
            jax.ShapeDtypeStruct((count, 192, 1024), kind) for count in shapes for kind in (jnp.bfloat16, jnp.float32)
        ),
        in_specs=[pl.BlockSpec(memory_space=pltpu.VMEM)] * len(operands),
        out_specs=(pl.BlockSpec(memory_space=pltpu.VMEM),) * (2 * len(shapes)),
        compiler_params=pltpu.CompilerParams(vmem_limit_bytes=32 * 1024 * 1024),
        cost_estimate=pl.CostEstimate(flops=flops, bytes_accessed=6_000_000, transcendentals=0),
    )(*operands)


def arrange_kernel(source_ref, rows_ref, out_ref):
    column = lax.broadcasted_iota(jnp.int32, (384, 128), 1)
    source = source_ref[...]
    total = None
    for at in range(3):
        term = dot(ones_where(source == column + 128 * at), rows_ref[at].reshape(128, 832))
        total = term if total is None else total + term
    out_ref[...] = total.astype(jnp.bfloat16)


def arrange(source, rows):
    return pl.pallas_call(
        arrange_kernel,
        out_shape=jax.ShapeDtypeStruct((384, 832), jnp.bfloat16),
        in_specs=[pl.BlockSpec(memory_space=pltpu.VMEM)] * 2,
        out_specs=pl.BlockSpec(memory_space=pltpu.VMEM),
        compiler_params=pltpu.CompilerParams(vmem_limit_bytes=16 * 1024 * 1024),
        cost_estimate=pl.CostEstimate(flops=20000000000, bytes_accessed=1_500_000, transcendentals=0),
    )(source, rows)


def quantize_weight(weight_matrix, weight_exponent):
    coarse = (weight_exponent == -8)[None, :]
    scaling = jnp.where(coarse, 2.0**-8, 2.0**-9)
    clipped = jnp.clip(weight_matrix.astype(jnp.float32) * jnp.where(coarse, 2.0**8, 2.0**9), -7.5, 7.5)
    return (soft_round(clipped) * scaling).astype(jnp.bfloat16)


def ring(size, shift):
    return [(at, (at + shift) % size) for at in range(size)]


def final_pairs(which):
    pairs = []
    for x in range(4):
        for slot in range(4):
            for y in range(8):
                for c in range(2):
                    first = 3 * (2 * y + c)
                    if which == "main":
                        k = (first + 1) // 16
                    elif first // 16 != (first + 1) // 16:
                        k = first // 16
                    elif (first + 2) // 16 != (first + 1) // 16:
                        k = (first + 2) // 16
                    else:
                        continue
                    owner_l = (4 * ((k - x) % 3) + x) // 3
                    owner_x = (x + SLOTS[slot]) % 4
                    source = ((x * 4 + slot) * 8 + y) * 2 + c
                    pairs.append((source, ((owner_x * 4 + owner_l) * 8 + y) * 2 + c))
    return pairs


def row_order(x, y_low, c):
    at = lax.broadcasted_iota(jnp.int32, (384, 1), 0)
    core = jnp.where(at < 192, 1 - c, c)
    rest = at % 192
    parity = jnp.where(rest < 96, 1 - y_low, y_low)
    rest = rest % 96
    y = 2 * (rest // 24) + parity
    row = (2 * y + core) * 24 + rest % 24
    return row % 128 + 128 * ((row // 128 - x + 6) % 3)


def shards(hidden, down_weight, act_exponent, clip_index, weight_exponent):
    x, y_low, c = (lax.axis_index(name) for name in ("x", "yl", "c"))
    y_high = lax.axis_index("yh")

    def to_right(rows):
        return lax.ppermute(rows, "x", ring(4, 1))

    def to_left(rows):
        return lax.ppermute(rows, "x", ring(4, -1))

    packed = pack(hidden, act_exponent, clip_index)
    packed, down_weight = lax.optimization_barrier((packed, down_weight))
    weight_0 = quantize_weight(down_weight, weight_exponent)
    weight_1, weight_3 = to_left(weight_0), to_right(weight_0)
    arrived = lax.all_to_all(packed, TENSOR, split_axis=0, concat_axis=0, tiled=True)
    quantized = rotate_and_quantize(arrived)
    own = lax.all_to_all(quantized, TENSOR, split_axis=0, concat_axis=0, tiled=True)
    rows = lax.all_to_all(
        jnp.broadcast_to(own[None], (3, 64, 2, 832)), "h", split_axis=0, concat_axis=0, tiled=True
    )
    weight_2 = (to_right(take_rows(weight_3, 0, SPLIT)), to_left(take_rows(weight_1, SPLIT, 832)))
    acts = arrange(row_order(x, y_low, c), rows)

    y_pairs_near = [(y, y ^ 1) for y in range(8)]
    y_pairs_far = [(y, (y - 1) % 8 if y % 2 == 0 else (y + 1) % 8) for y in range(8)]
    def over_core(other, own_rows):
        return own_rows + lax.ppermute(other, "c", [(0, 1), (1, 0)]).astype(jnp.float32)

    def over_y(mine, y_pairs):
        from_y = lax.ppermute(mine[:, :96].astype(jnp.bfloat16), ("yh", "yl"), y_pairs)
        return (mine[:, 96:] + from_y.astype(jnp.float32)).astype(jnp.bfloat16)

    other, own_rows, far_other, far_rows = products(
        first_kernel, (2, 1), (acts, weight_0, weight_1, weight_3), 1_300_000_000
    )
    near = over_core(other, own_rows)
    far_other, far_rows = products(last_kernel, (2,), (acts, *weight_2, far_other, far_rows), 1_300_000_000)
    far = over_core(far_other, far_rows)
    parts = [over_y(near, y_pairs_near), over_y(far, y_pairs_far)]
    sums = jnp.concatenate(parts, axis=0).reshape(16, 24, 1024)
    crossed = lax.all_to_all(sums, ("l", "yh"), split_axis=0, concat_axis=0, tiled=True)
    total = jnp.sum(crossed.astype(jnp.float32), axis=0).astype(jnp.bfloat16)

    y = 2 * y_high + y_low
    early = jnp.logical_and(y == 2, c == 1)
    late = jnp.logical_and(y == 5, c == 0)
    moved = lax.ppermute(total, ("x", "l", "yh", "yl", "c"), final_pairs("main"))
    fixed = lax.ppermute(
        jnp.where(early, total[:8], total[16:]), ("x", "l", "yh", "yl", "c"), final_pairs("fix")
    )
    return jnp.concatenate(
        [jnp.where(early, fixed, moved[:8]), moved[8:16], jnp.where(late, fixed, moved[16:])], axis=0
    )


def solution(mesh):
    fine = Mesh(mesh.devices.reshape(SIZES), AXES)
    rows, columns = ("h", "x"), TENSOR
    placed = (P(rows, columns), P(columns, rows), P(rows, columns), P(columns), P(rows))
    return jax.shard_map(
        shards, mesh=fine, in_specs=placed, out_specs=P(columns, rows), check_vma=False
    )
```
